32 devices in a mesh: space: 8 (over z, x), chan: 4 (over y, core).
Axes of the slice: x: 2, y: 2, z: 4, core: 2. Of those that a mesh axis runs over, the one named last changes fastest.
Arguments:
- features: bfloat16 [128, 2048], P('chan', 'space'), may hold values from -6 to 6
- positions: float32 [3, 2048], P(None, 'space'), may hold values from 0 to 16, as said below
- species: int32 [2048], P('space'), may hold values from 0 to 5
- block_count: int32 [32], P('space'), may hold values from 48 to 64, as said below
- pair_home: int32 [128], P('space'), may hold values from 0 to 3, as said below
- pair_reach: int32 [128], P('space'), may hold values from 1 to 4, as said below
- pair_count: int32 [8], P('space'), may hold values from 4 to 16, as said below
- wave_ints: int32 [3, 1024], replicated, may hold values from -8 to 8, as said below
- species_gain: float32 [6, 128], P(None, 'chan'), may hold values from 0.5 to 2
- w_in: bfloat16 [128, 128], replicated, may hold values from -0.5 to 0.5
- w_rad: float32 [16, 128], P(None, 'chan'), may hold values from -1.5 to 1.5
- cotangent: bfloat16 [9, 128, 2048], P(None, 'chan', 'space'), may hold values from -6 to 6
Outputs:
- messages: bfloat16 [9, 128, 2048], P(None, 'chan', 'space')
- grad_features: float32 [128, 2048], P('chan', 'space')
The draws below stay inside these ranges and needn't reach their ends.
Inputs may be any that keep to these rules, and one draw needn't show every extreme that they name: `positions`: atom a lies in block a // 64: its first coordinate lies in [0.5 (a // 64), 0.5 (a // 64 + 1)); the other two lie in [0, 1.5). `block_count`: some block is full. `pair_home`: the 16 slots of one index of space hold every pair (home, reach) with home in 0..3 and reach in 1..4 exactly once, in an order drawn from the seed. `pair_reach`: as for pair_home, the same slots. `pair_count`: live slots come first; some index of space has all 16 live. `wave_ints`: no wavevector is all zeros; the first component lies in -8..8, the others in -4..4.
All inputs are finite; a program needn't handle non-finite values.
Results may differ from the reference program's by a relative error of at most 0.0051.
Values may be sent and summed in bfloat16 or wider, within the bound.
No kernel may reach another device: no remote copies, remote signals or barrier semaphores. Data moves between devices by JAX's collectives and lax.ppermute only.
A program may use at most 64 MiB of HBM per device.

```python
import math
import jax
import jax.numpy as jnp
from jax import lax

C = 128
NRAD = 16
NHARM = 9
KVEC = 1024
NSPEC = 6
BLOCK = 64
REACH = 4
NB = 4
NBLOCKS = 32
ATOMS = 2048


def draw_positions(key, part):
    first, second, third = jax.random.split(key, 3)
    count = NBLOCKS * BLOCK
    atom_block = (jnp.arange(count, dtype=jnp.int32) // BLOCK).astype(jnp.float32)
    along = (atom_block + jax.random.uniform(first, (count,), jnp.float32)) * 0.5
    across = jax.random.uniform(second, (count,), jnp.float32) * 1.5
    height = jax.random.uniform(third, (count,), jnp.float32) * 1.5
    return jnp.stack([along, across, height])


def draw_w_rad(key, part):
    key = jax.random.fold_in(key, 13)
    first, second = jax.random.split(key)
    rows = jnp.arange(NRAD, dtype=jnp.int32)[:, None]
    strong = jnp.logical_and(rows >= NRAD - 5, rows <= NRAD - 2)
    wide = jax.random.uniform(first, (NRAD, C), jnp.float32, -1.5, 1.5)
    faint = jnp.clip(jax.random.normal(second, (NRAD, C), jnp.float32) * 0.02, -0.12, 0.12)
    return jnp.where(strong, wide, faint).astype(jnp.float32)


def draw_block_count(key, part):
    first, second = jax.random.split(jax.random.fold_in(key, 3))
    counts = jax.random.randint(first, (NBLOCKS,), BLOCK - BLOCK // 4, BLOCK + 1)
    full = jax.random.randint(second, (), 0, NBLOCKS)
    return jnp.where(jnp.arange(NBLOCKS) == full, BLOCK, counts).astype(jnp.int32)


def pair_listing(key):
    base = jax.random.fold_in(key, 7)
    slots = NB * REACH
    devices = NBLOCKS // NB

    def one_index(index):
        return jax.random.permutation(jax.random.fold_in(base, index), slots)
    order = jax.vmap(one_index)(jnp.arange(devices, dtype=jnp.int32))
    return order.reshape(-1).astype(jnp.int32)


def draw_pair_home(key, part):
    return (pair_listing(key) // REACH).astype(jnp.int32)


def draw_pair_reach(key, part):
    return (pair_listing(key) % REACH + 1).astype(jnp.int32)


def draw_pair_count(key, part):
    slots = NB * REACH
    devices = NBLOCKS // NB
    first, second, third = jax.random.split(jax.random.fold_in(key, 11), 3)
    modest = jax.random.randint(first, (devices,), slots // 4, slots // 2 + 1)
    busy = jax.random.randint(second, (devices,), 0, 8) == 0
    full = jax.random.randint(third, (), 0, devices)
    chosen = jnp.logical_or(busy, jnp.arange(devices) == full)
    return jnp.where(chosen, slots, modest).astype(jnp.int32)


def draw_wave_ints(key, part):
    first, second, third = jax.random.split(jax.random.fold_in(key, 5), 3)
    along = jax.random.randint(first, (KVEC,), -8, 9)
    across = jax.random.randint(second, (KVEC,), -4, 5)
    height = jax.random.randint(third, (KVEC,), -4, 5)
    empty = jnp.logical_and(jnp.logical_and(along == 0, across == 0), height == 0)
    height = jnp.where(empty, 1, height)
    return jnp.stack([along, across, height]).astype(jnp.int32)


def plant(values, own_key, least, high):
    shape = values.shape
    place = [jax.random.randint(jax.random.fold_in(own_key, axis), (), 0, shape[axis]) for axis in range(len(shape))]
    values = values.at[tuple(place)].set(least)
    longest = shape.index(max(shape))
    place[longest] = (place[longest] + 1) % shape[longest]
    return values.at[tuple(place)].set(high)


def level_of(key, extent, cuts, low, high):
    def one(dim, shards_of):
        draws = jax.random.uniform(jax.random.fold_in(jax.random.fold_in(key, 6), dim), (shards_of,), jnp.float32, low / len(cuts), high / len(cuts))
        return jnp.repeat(jnp.exp(draws), extent[dim] // shards_of).reshape((-1,) + (1,) * (len(extent) - dim - 1))

    level = one(*cuts[0])
    for cut in cuts[1:]:
        level = level * one(*cut)
    return level


def gaussian(stream_key, extent, width, bound, shards=(), kind=jnp.bfloat16):
    result = jax.random.normal(stream_key, extent, jnp.float32) * width
    if len(shards) > 0:
        result = level_of(stream_key, extent, shards, -0.22, 0.18) * result
    return jnp.clip(result, min=-bound, max=bound).astype(kind)


def setup_inputs(seed: int = 0) -> dict:
    key_list = jax.random.split(jax.random.key(seed), 13)
    features = gaussian(key_list[0], (C, ATOMS), 1.0, 6.0, ((0, 4), (1, 8)))
    positions = draw_positions(jax.random.fold_in(key_list[12], 71), 0)
    species = plant(jax.random.randint(key_list[2], (ATOMS,), 0, NSPEC), jax.random.fold_in(key_list[2], 1), 0, NSPEC - 1).astype(jnp.int32)
    block_count = draw_block_count(jax.random.fold_in(key_list[12], 71), 0)
    pair_home = draw_pair_home(jax.random.fold_in(key_list[12], 71), 0)
    pair_reach = draw_pair_reach(jax.random.fold_in(key_list[12], 71), 0)
    pair_count = draw_pair_count(jax.random.fold_in(key_list[12], 71), 0)
    wave_ints = draw_wave_ints(jax.random.fold_in(key_list[12], 71), 0)
    species_gain = jnp.clip(0.5 + 1.5 * jax.random.uniform(key_list[8], (NSPEC, C), jnp.float32) ** level_of(key_list[8], (NSPEC, C), ((1, 4),), -0.2, 0.2), 0.5, 2.0)
    w_in = gaussian(key_list[9], (C, C), C ** -0.5, 0.5)
    w_rad = draw_w_rad(jax.random.fold_in(key_list[12], 71), 0)
    cotangent = gaussian(key_list[11], (NHARM, C, ATOMS), 1.0, 6.0, ((1, 4), (2, 8)))
    return {"features": features, "positions": positions, "species": species, "block_count": block_count, "pair_home": pair_home, "pair_reach": pair_reach, "pair_count": pair_count, "wave_ints": wave_ints, "species_gain": species_gain, "w_in": w_in, "w_rad": w_rad, "cotangent": cotangent}


SLICE_WIDTH = 0.5
SIDE_WIDTH = 12.0
GAP_HEIGHT = 24.0
SCREEN = 0.5
HARM_SIGNS = (1.0, -1.0, -1.0, -1.0, 1.0, 1.0, 1.0, 1.0, 1.0)
HIGH = lax.Precision.HIGHEST

def harmonics(unit):
    ux, uy, uz = (unit[0], unit[1], unit[2])
    squared = ux * ux + uy * uy + uz * uz
    root_three = math.sqrt(3.0)
    root_fifteen = math.sqrt(15.0)
    root_five = math.sqrt(5.0)
    return jnp.stack([jnp.ones_like(ux), root_three * ux, root_three * uy, root_three * uz, root_fifteen * ux * uy, root_fifteen * uy * uz, 0.5 * root_five * (3.0 * uz * uz - squared), root_fifteen * ux * uz, 0.5 * root_fifteen * (ux * ux - uy * uy)])

def pair_terms(pos_home, pos_far, data_home, data_far, w_rad, cutoff, self_pair):
    disp = pos_far[:, None, :] - pos_home[:, :, None]
    unit = disp / cutoff
    squared = unit[0] * unit[0] + unit[1] * unit[1] + unit[2] * unit[2]
    envelope = jnp.square(jnp.maximum(1.0 - squared, 0.0))
    count = w_rad.shape[0]
    centres = jnp.arange(count).astype(jnp.float32) / (count - 1)
    gamma = 0.5 * (count - 1) ** 2
    radial = envelope[None] * jnp.exp(-gamma * jnp.square(squared[None] - centres[:, None, None]))
    if self_pair:
        radial = radial * (1.0 - jnp.eye(pos_home.shape[1], dtype=jnp.float32))[None]
    filt = jnp.einsum('rc,rij->cij', w_rad, radial, precision=HIGH)
    harm = harmonics(unit)
    signed = harm * jnp.array(HARM_SIGNS, jnp.float32)[:, None, None]
    source_home = data_home[0].astype(jnp.float32)
    source_far = data_far[0].astype(jnp.float32)
    grad_home = data_home[1:].astype(jnp.float32)
    grad_far = data_far[1:].astype(jnp.float32)
    home_msg = jnp.einsum('lij,cij->lci', harm, filt * source_far[:, None, :], precision=HIGH)
    far_dx = lax.optimization_barrier(jnp.sum(filt * jnp.einsum('lij,lci->cij', harm, grad_home, precision=HIGH), axis=1))
    far_msg = jnp.einsum('lij,cij->lcj', signed, filt * source_home[:, :, None], precision=HIGH)
    home_dx = lax.optimization_barrier(jnp.sum(filt * jnp.einsum('lij,lcj->cij', signed, grad_far, precision=HIGH), axis=2))
    return (home_msg, far_dx, far_msg, home_dx)

def add_block(total, update, start):
    current = lax.dynamic_slice_in_dim(total, start, update.shape[2], 2)
    return lax.dynamic_update_slice_in_dim(total, current + update, start, 2)

def wave_table(positions, wave_ints, length):
    box = jnp.array([length, SIDE_WIDTH, GAP_HEIGHT], jnp.float32)
    freq = 2.0 * math.pi * wave_ints.astype(jnp.float32) / box[:, None]
    angle = freq[0][:, None] * positions[0][None, :] + freq[1][:, None] * positions[1][None, :]
    angle = angle + freq[2][:, None] * positions[2][None, :]
    return jnp.concatenate([jnp.cos(angle), jnp.sin(angle)], 0).astype(jnp.bfloat16)

def wave_weight(wave_ints, length):
    box = jnp.array([length, SIDE_WIDTH, GAP_HEIGHT], jnp.float32)
    freq = 2.0 * math.pi * wave_ints.astype(jnp.float32) / box[:, None]
    ksq = freq[0] * freq[0] + freq[1] * freq[1] + freq[2] * freq[2]
    value = jnp.exp(-0.5 * ksq) / (ksq + SCREEN * SCREEN)
    return jnp.concatenate([value, value], 0)

def reference(features, positions, species, block_count, pair_home, pair_reach, pair_count, wave_ints, species_gain, w_in, w_rad, cotangent):
    atoms = features.shape[1]
    nblocks = atoms // BLOCK
    length = SLICE_WIDTH * nblocks
    cutoff = SLICE_WIDTH * REACH
    slots = NB * REACH
    valid = (jnp.arange(atoms).astype(jnp.int32) % BLOCK < jnp.repeat(block_count, BLOCK)).astype(jnp.float32)
    onehot = (species[None, :] == jnp.arange(NSPEC).astype(jnp.int32)[:, None]).astype(jnp.float32)
    gain = jnp.dot(species_gain.T, onehot, precision=HIGH)
    mixed = jnp.dot(w_in.T, features, preferred_element_type=jnp.float32)
    source = (mixed * gain * valid).astype(jnp.bfloat16)
    grad_in = cotangent * valid.astype(jnp.bfloat16)[None, None, :]
    table = wave_table(positions, wave_ints, length)
    weight = wave_weight(wave_ints, length) * (1.0 / math.sqrt(KVEC * atoms))
    sums = jnp.dot(table, source.T, preferred_element_type=jnp.float32)
    grads = jnp.dot(table, grad_in[0].T, preferred_element_type=jnp.float32)
    far_field = jnp.dot((sums * weight[:, None]).astype(jnp.bfloat16).T, table, preferred_element_type=jnp.float32)
    far_grad = jnp.dot((grads * weight[:, None]).astype(jnp.bfloat16).T, table, preferred_element_type=jnp.float32)
    stacked = jnp.concatenate([source[None], grad_in], 0)
    x_unit = jnp.array([1.0, 0.0, 0.0], jnp.float32)[:, None]

    def self_step(total, block):
        start = block * BLOCK
        pos = lax.dynamic_slice_in_dim(positions, start, BLOCK, 1)
        data = lax.dynamic_slice_in_dim(stacked, start, BLOCK, 2)
        home_msg, far_dx, far_msg, home_dx = pair_terms(pos, pos, data, data, w_rad, cutoff, True)
        return (add_block(total, jnp.concatenate([home_msg, far_dx[None]], 0), start), None)
    total = jnp.zeros((cotangent.shape[0] + 1, features.shape[0], atoms), jnp.float32)
    total, unused = lax.scan(self_step, total, jnp.arange(nblocks).astype(jnp.int32))
    slot = jnp.arange(nblocks * REACH).astype(jnp.int32)
    owner = slot // slots
    live = (slot % slots < pair_count[owner]).astype(jnp.float32)
    home = owner * NB + pair_home
    far_raw = home + pair_reach
    wrapped = (far_raw >= nblocks).astype(jnp.int32)
    far = far_raw - nblocks * wrapped
    offset = wrapped.astype(jnp.float32) * length

    def cross_step(total, item):
        home_block, far_block, shift, alive = item
        home_start = home_block * BLOCK
        far_start = far_block * BLOCK
        pos_home = lax.dynamic_slice_in_dim(positions, home_start, BLOCK, 1)
        pos_far = lax.dynamic_slice_in_dim(positions, far_start, BLOCK, 1) + shift * x_unit
        data_home = lax.dynamic_slice_in_dim(stacked, home_start, BLOCK, 2)
        data_far = lax.dynamic_slice_in_dim(stacked, far_start, BLOCK, 2)
        home_msg, far_dx, far_msg, home_dx = pair_terms(pos_home, pos_far, data_home, data_far, w_rad, cutoff, False)
        total = add_block(total, alive * jnp.concatenate([home_msg, home_dx[None]], 0), home_start)
        total = add_block(total, alive * jnp.concatenate([far_msg, far_dx[None]], 0), far_start)
        return (total, None)
    total, unused = lax.scan(cross_step, total, (home, far, offset, live))
    first = total[0] + far_field
    messages = (jnp.concatenate([first[None], total[1:9]], 0) * valid).astype(jnp.bfloat16)
    scaled = ((total[9] + far_grad) * gain * valid).astype(jnp.bfloat16)
    grad_features = jnp.dot(w_in, scaled, preferred_element_type=jnp.float32)
    return (messages, grad_features)
```

```python
import functools
import math

import jax
import jax.numpy as jnp
from jax import lax
from jax.experimental import pallas as pl
from jax.experimental.pallas import tpu as pltpu
from jax.sharding import PartitionSpec as P

NSPEC = 6
BLOCK = 64
REACH = 4
NRAD = 16
NHARM = 9
KLONG = 8
KMODE = 128
MID = NRAD // 2

SLICE_WIDTH = 0.5
CUTOFF = SLICE_WIDTH * REACH
SIDE_WIDTH = 12.0
GAP_HEIGHT = 24.0
SIDE_CENTRE = 0.75
SCREEN = 0.5
HIGH = lax.Precision.HIGHEST
BF = jnp.bfloat16
F32 = jnp.float32
R3 = math.sqrt(3.0)
R5 = math.sqrt(5.0)
R15 = math.sqrt(15.0)

VMEM = pl.BlockSpec(memory_space=pltpu.VMEM)
SMEM = pl.BlockSpec(memory_space=pltpu.SMEM)


def dot_nt(a, b):
    return lax.dot_general(a, b, (((1,), (1,)), ((), ())), preferred_element_type=F32)


def dot_nn(a, b):
    return lax.dot_general(a, b, (((1,), (0,)), ((), ())), preferred_element_type=F32)


def harmonic_rows(x, y, z):
    s = x * x + y * y + z * z
    return [
        None,
        R3 * x,
        R3 * y,
        R3 * z,
        R15 * x * y,
        R15 * y * z,
        0.5 * R5 * (3.0 * z * z - s),
        R15 * x * z,
        0.5 * R15 * (x * x - y * y),
    ]


def shift_terms(x, y, z):
    q = R15 / R3
    return {
        (1, 0): -R3 * x,
        (2, 0): -R3 * y,
        (3, 0): -R3 * z,
        (4, 1): -q * y,
        (4, 2): -q * x,
        (4, 0): R15 * x * y,
        (5, 3): -q * y,
        (5, 2): -q * z,
        (5, 0): R15 * y * z,
        (6, 3): (-2.0 * R5 / R3) * z,
        (6, 1): (R5 / R3) * x,
        (6, 2): (R5 / R3) * y,
        (6, 0): 0.5 * R5 * (2.0 * z * z - x * x - y * y),
        (7, 3): -q * x,
        (7, 1): -q * z,
        (7, 0): R15 * x * z,
        (8, 1): -q * x,
        (8, 2): q * y,
        (8, 0): 0.5 * R15 * (x * x - y * y),
    }


def sincos_turns(turns):
    r = turns - jnp.floor(turns + 0.5)
    x = r * math.pi
    x2 = x * x
    s = jnp.full_like(x, -1.0 / math.factorial(11))
    for k, sign in ((9, 1.0), (7, -1.0), (5, 1.0), (3, -1.0), (1, 1.0)):
        s = s * x2 + sign / math.factorial(k)
    s = s * x
    c = jnp.full_like(x, 1.0 / math.factorial(12))
    for k, sign in ((10, -1.0), (8, 1.0), (6, -1.0), (4, 1.0), (2, -1.0), (0, 1.0)):
        c = c * x2 + sign / math.factorial(k)
    return 1.0 - 2.0 * s * s, 2.0 * s * c


def valid_row(count_ref, atoms):
    lane = lax.broadcasted_iota(jnp.int32, (1, atoms), 1)
    limit = jnp.zeros((1, atoms), jnp.int32)
    for b in range(atoms // BLOCK):
        limit = jnp.where(lane // BLOCK == b, count_ref[b] + b * BLOCK, limit)
    return (lane < limit).astype(F32)


def gain_rows(species_ref, species_gain_ref):
    ids = species_ref[...]
    rows = lax.broadcasted_iota(jnp.int32, (8, ids.shape[1]), 0)
    onehot = (rows == ids).astype(F32)[:NSPEC]
    return lax.dot_general(
        species_gain_ref[...],
        onehot,
        (((0,), (0,)), ((), ())),
        precision=HIGH,
        preferred_element_type=F32,
    )


def source_kernel(
    count_ref,
    home_ref,
    reach_ref,
    live_ref,
    lane_ref,
    features_ref,
    w_ref,
    species_ref,
    gain_ref,
    pos_ref,
    cot_ref,
    pack_ref,
    mix_ref,
):
    channels, atoms = cot_ref.shape[1], cot_ref.shape[2]
    valid = valid_row(count_ref, atoms)
    gain = gain_rows(species_ref, gain_ref)
    mix_ref[...] = lax.dot_general(
        w_ref[...], features_ref[...], (((0,), (0,)), ((), ())), preferred_element_type=F32
    )
    first = pl.multiple_of(lane_ref[0] * channels, channels)
    mixed = mix_ref[pl.ds(first, channels), :]
    pack_ref[0:channels, :] = (mixed * gain * valid).astype(BF)
    pack_ref[channels : 2 * channels, :] = (cot_ref[0].astype(F32) * valid).astype(BF)
    pos = pos_ref[...]
    top = pos.astype(BF).astype(F32)
    rest = pos - top
    mid = rest.astype(BF).astype(F32)
    low = rest - mid
    lane = lax.broadcasted_iota(jnp.int32, (1, atoms), 1)
    flags = jnp.zeros((1, atoms), F32)
    for p in range(home_ref.shape[0]):
        slot = home_ref[p] * REACH + reach_ref[p] - 1
        flags = jnp.where(jnp.logical_and(lane == slot, p < live_ref[0]), 1.0, flags)
    tail = jnp.concatenate([top, mid, low, flags, valid, jnp.zeros((5, atoms), F32)], 0)
    pack_ref[2 * channels :, :] = tail.astype(BF)


def mode_weights(wave_ref, length, total):
    k = wave_ref[...]
    count = k.shape[1]
    k = jnp.where(k[0:1] < 0, -k, k)
    k1, k2, k3 = k[0:1], k[1:2], k[2:3]
    code = jnp.where(k3 == 4, 76 + k2, (k2 + 4) * 8 + k3 + 4)
    rows = lax.broadcasted_iota(jnp.int32, (KMODE, count), 0)
    hot = (rows == code).astype(F32).astype(BF)
    longs = lax.broadcasted_iota(jnp.int32, (16, count), 0)
    hot1 = (longs == k1).astype(F32).astype(BF)
    mult = dot_nt(hot1, hot)
    lane = lax.broadcasted_iota(jnp.int32, (16, KMODE), 1)
    row = lax.broadcasted_iota(jnp.int32, (16, KMODE), 0)
    g2 = jnp.where(lane < 72, lane // 8 - 4, lane - 76).astype(F32)
    g3 = jnp.where(lane < 72, lane % 8 - 4, 4).astype(F32)
    f1 = row.astype(F32) * (2.0 * math.pi / length)
    f2 = g2 * (2.0 * math.pi / SIDE_WIDTH)
    f3 = g3 * (2.0 * math.pi / GAP_HEIGHT)
    ksq = f1 * f1 + f2 * f2 + f3 * f3
    value = jnp.exp(-0.5 * ksq) / (ksq + SCREEN * SCREEN) * (1.0 / math.sqrt(count * total))
    return jnp.where(mult > 0.0, mult * value, 0.0)


def phase_rows(x, y, z, length):
    atoms = x.shape[1]
    step = lax.broadcasted_iota(jnp.int32, (8, atoms), 0).astype(F32)
    first = sincos_turns((step + 1.0) * (x * (1.0 / length)))
    second = sincos_turns((step - 4.0) * (y * (1.0 / SIDE_WIDTH)))
    third = sincos_turns((step - 4.0) * (z * (1.0 / GAP_HEIGHT)))
    return first, second, third


def mode_table(second, third):
    c2, s2 = second
    c3, s3 = third
    atoms = c2.shape[1]
    cos, sin = [], []
    for k2 in range(9):
        a = c2[k2 : k2 + 1] if k2 < 8 else c2[0:1]
        b = s2[k2 : k2 + 1] if k2 < 8 else -s2[0:1]
        cos.append(a * c3 - b * s3)
        sin.append(a * s3 + b * c3)
    a, b = c3[0:1], -s3[0:1]
    cos.append(c2 * a - s2 * b)
    sin.append(c2 * b + s2 * a)
    one = lax.broadcasted_iota(jnp.int32, (8, atoms), 0) == 0
    cos.append(jnp.where(one, c2[0:1] * a + s2[0:1] * b, 0.0))
    sin.append(jnp.where(one, c2[0:1] * b - s2[0:1] * a, 0.0))
    pad = jnp.zeros((KMODE - 88, atoms), F32)
    return jnp.concatenate(cos + [pad] + sin + [pad], 0).astype(BF)


def unpack_pos(tail):
    t = tail.astype(F32)
    pos = (t[0:3] + t[3:6]) + t[6:9]
    return pos[0:1], pos[1:2], pos[2:3]


def far_part(spaces, length, wave_ref, gath_ref, terms_ref, modes_ref, rows_per):
    atoms = gath_ref.shape[2]
    group = min(spaces, modes_ref.shape[1] // atoms)
    weights = mode_weights(wave_ref, length, atoms * spaces)

    def fill(s, base):
        tile = gath_ref[base + s]
        x, y, z = unpack_pos(tile[rows_per : rows_per + 16])
        first, second, third = phase_rows(x, y, z, length)
        at = pl.ds(pl.multiple_of(s * atoms, atoms), atoms)
        modes_ref[:, at] = mode_table(second, third)
        data = tile[0:rows_per].astype(F32)
        terms_ref[0:rows_per, at] = tile[0:rows_per]
        for k in range(KLONG):
            lo = (1 + 2 * k) * rows_per
            terms_ref[lo : lo + rows_per, at] = (data * first[0][k : k + 1]).astype(BF)
            terms_ref[lo + rows_per : lo + 2 * rows_per, at] = (
                data * first[1][k : k + 1]
            ).astype(BF)
        return base

    sums = None
    for base in range(0, spaces, group):
        lax.fori_loop(0, group, fill, base)
        part = dot_nt(terms_ref[...], modes_ref[...])
        sums = part if sums is None else sums + part
    tile = gath_ref[0]
    x, y, z = unpack_pos(tile[rows_per : rows_per + 16])
    first, second, third = phase_rows(x, y, z, length)
    own = mode_table(second, third)
    rows_re, rows_im = [], []
    for k in range(KLONG + 1):
        w = weights[k : k + 1]
        if k == 0:
            real = sums[0:rows_per]
            cos, sin = real[:, :KMODE], real[:, KMODE:]
        else:
            lo = (2 * k - 1) * rows_per
            real, imag = sums[lo : lo + rows_per], sums[lo + rows_per : lo + 2 * rows_per]
            cos = real[:, :KMODE] - imag[:, KMODE:]
            sin = real[:, KMODE:] + imag[:, :KMODE]
        cos, sin = cos * w, sin * w
        rows_re.append(jnp.concatenate([cos, sin], 1))
        if k > 0:
            rows_im.append(jnp.concatenate([sin, -cos], 1))
    waves = jnp.concatenate(rows_re + rows_im, 0).astype(BF)
    back = dot_nn(waves, own)
    far = back[0:rows_per]
    for k in range(KLONG):
        lo = (1 + k) * rows_per
        far = far + back[lo : lo + rows_per] * first[0][k : k + 1]
        lo = (1 + KLONG + k) * rows_per
        far = far + back[lo : lo + rows_per] * first[1][k : k + 1]
    return far


def main_kernel(
    spaces,
    place_ref,
    gath_ref,
    cot_prev_ref,
    cot_ref,
    cot_next_ref,
    wave_ref,
    w_rad_ref,
    species_ref,
    gain_ref,
    messages_ref,
    scaled_ref,
    radial_ref,
    left_ref,
    cols_ref,
    live_ref,
    filt_ref,
    total_ref,
    terms_ref,
    modes_ref,
):
    channels, atoms = cot_ref.shape[1], cot_ref.shape[2]
    blocks = atoms // BLOCK
    rows = 2 * channels
    length = SLICE_WIDTH * blocks * spaces
    place = place_ref[0]
    before = lax.rem(place + spaces - 1, spaces)
    after = lax.rem(place + 1, spaces)
    tiles = [gath_ref[before ^ place], gath_ref[0], gath_ref[after ^ place]]
    shifts = [
        jnp.where(place == 0, -length, 0.0),
        0.0,
        jnp.where(place == spaces - 1, length, 0.0),
    ]
    centre = (place.astype(F32) + 0.5) * (SLICE_WIDTH * blocks)
    lane = lax.broadcasted_iota(jnp.int32, (1, atoms), 1)
    home = lane // BLOCK

    def flag_row(tail, h, r):
        index = h * REACH + r - 1
        return jnp.broadcast_to(tail[9:10, index : index + 1].astype(F32), (1, atoms))

    coords, valids = [], []
    for t in range(3):
        tail = tiles[t][rows : rows + 16]
        x, y, z = unpack_pos(tail)
        x = (x - (centre - shifts[t])) * (1.0 / CUTOFF)
        y = (y - SIDE_CENTRE) * (1.0 / CUTOFF)
        z = (z - SIDE_CENTRE) * (1.0 / CUTOFF)
        coords.append((x, y, z))
        valids.append(tail[10:11].astype(F32))
        padded = jnp.concatenate([x, y, z, jnp.zeros((5, atoms), F32)], 0)
        cols_ref[t * atoms : (t + 1) * atoms, :] = padded.T
    for e in range(3 * blocks):
        row = jnp.zeros((1, atoms), F32)
        for h in range(blocks):
            d = e - blocks - h
            if abs(d) > REACH:
                continue
            if d == 0:
                value = jnp.ones((1, atoms), F32)
            elif d > 0:
                value = flag_row(tiles[1][rows : rows + 16], h, d)
            elif h + d >= 0:
                value = flag_row(tiles[1][rows : rows + 16], h + d, -d)
            else:
                value = flag_row(tiles[0][rows : rows + 16], h + d + blocks, -d)
            row = jnp.where(home == h, value, row)
        live_ref[e : e + 1, :] = row

    w_cols = w_rad_ref[...].T
    for n in range(NRAD):
        filt_ref[n] = jnp.broadcast_to(w_cols[:, n : n + 1], (channels, atoms))

    for t, cot in enumerate((cot_prev_ref, cot_ref, cot_next_ref)):
        x, y, z = coords[t]
        at = slice(t * atoms, (t + 1) * atoms)
        left_ref[0:channels, at] = tiles[t][0:channels]
        source = tiles[t][0:channels].astype(F32)
        harm = harmonic_rows(x, y, z)
        for m in range(1, NHARM):
            left_ref[m * channels : (m + 1) * channels, at] = (source * harm[m]).astype(BF)
        grads = [cot[l].astype(F32) * valids[t] for l in range(NHARM)]
        moved = list(grads)
        for (l, m), term in shift_terms(x, y, z).items():
            moved[m] = moved[m] + grads[l] * term
        for m in range(NHARM):
            lo = (NHARM + m) * channels
            left_ref[lo : lo + channels, at] = moved[m].astype(BF)

    xa, ya, za = coords[1]
    chunk = 16

    def radial_step(step, carry):
        lo = pl.multiple_of(step * chunk, chunk)
        at = pl.ds(lo, chunk)
        col = cols_ref[at, :]
        dx = col[:, 0:1] - xa
        dy = col[:, 1:2] - ya
        dz = col[:, 2:3] - za
        s = jnp.minimum(dx * dx + dy * dy + dz * dz, 1.0)
        live = live_ref[pl.ds(lo // BLOCK, 1), :]
        other = lax.broadcasted_iota(jnp.int32, (chunk, atoms), 0) + (lo - atoms)
        me = lax.broadcasted_iota(jnp.int32, (chunk, atoms), 1)
        gap = 1.0 - s
        envelope = jnp.where(other == me, 0.0, gap * gap * live)
        off = s - MID / (NRAD - 1)
        middle = envelope * jnp.exp(-0.5 * (NRAD - 1) ** 2 * (off * off))
        radial_ref[MID, at, :] = middle.astype(BF)
        grow = jnp.exp((NRAD - 1.0) * s)
        value = middle
        for n in range(MID, NRAD - 1):
            value = value * (grow * math.exp(-(2 * n + 1) / 2))
            radial_ref[n + 1, at, :] = value.astype(BF)
        shrink = jnp.exp((1.0 - NRAD) * s)
        value = middle
        for n in range(MID, 0, -1):
            value = value * (shrink * math.exp((2 * n - 1) / 2))
            radial_ref[n - 1, at, :] = value.astype(BF)
        return carry

    lax.fori_loop(0, 3 * atoms // chunk, radial_step, 0)

    total_ref[...] = jnp.zeros_like(total_ref)

    def mix_step(n, carry):
        part = dot_nn(left_ref[...], radial_ref[n])
        total_ref[...] += part.reshape(2 * NHARM, channels, atoms) * filt_ref[n][None]
        return carry

    lax.fori_loop(0, NRAD, mix_step, 0)

    far = far_part(spaces, length, wave_ref, gath_ref, terms_ref, modes_ref, rows)
    valid = valids[1]
    sums = [total_ref[m] for m in range(NHARM)]
    near = list(sums)
    for (l, m), term in shift_terms(xa, ya, za).items():
        near[l] = near[l] + sums[m] * term
    near[0] = near[0] + far[0:channels]
    for l in range(NHARM):
        messages_ref[l] = (near[l] * valid).astype(BF)
    harm = harmonic_rows(xa, ya, za)
    grad = total_ref[NHARM] + far[channels:rows]
    for m in range(1, NHARM):
        grad = grad + total_ref[NHARM + m] * harm[m]
    gain = gain_rows(species_ref, gain_ref)
    scaled_ref[...] = (grad * gain * valid).astype(BF)


def final_kernel(lane_ref, w_ref, scaled_ref, out_ref):
    channels = out_ref.shape[0]
    first = pl.multiple_of(lane_ref[0] * channels, channels)
    out_ref[...] = dot_nn(w_ref[pl.ds(first, channels), :], scaled_ref[...])


def gathered(pack, axis):
    count = lax.axis_size(axis)
    held = pack[None]
    bit = 1
    while bit < count:
        other = lax.ppermute(held, axis, [(i, i ^ bit) for i in range(count)])
        held = jnp.concatenate([held, other], 0)
        bit *= 2
    return held


def passed_along(block, axis, distance):
    count = lax.axis_size(axis)
    return lax.ppermute(block, axis, [((i - distance) % count, i) for i in range(count)])


def on_device(
    features,
    positions,
    species,
    block_count,
    pair_home,
    pair_reach,
    pair_count,
    wave_ints,
    species_gain,
    w_in,
    w_rad,
    cotangent,
):
    channels, atoms = features.shape
    spaces = lax.axis_size("space")
    place = lax.axis_index("space").astype(jnp.int32).reshape(1)
    lane = lax.axis_index("chan").astype(jnp.int32).reshape(1)
    params = pltpu.CompilerParams(vmem_limit_bytes=48 * 1024 * 1024)
    rows = 2 * channels
    species = species.reshape(1, atoms)

    cot_prev = passed_along(cotangent, "space", 1)
    cot_next = passed_along(cotangent, "space", -1)
    mixed_from = lax.all_gather(features, "chan", axis=0, tiled=True)
    pack = pl.pallas_call(
        source_kernel,
        out_shape=jax.ShapeDtypeStruct((rows + 16, atoms), BF),
        in_specs=[SMEM] * 5 + [VMEM] * 6,
        out_specs=VMEM,
        scratch_shapes=[pltpu.VMEM((w_in.shape[1], atoms), F32)],
        compiler_params=params,
        name="source",
    )(
        block_count,
        pair_home,
        pair_reach,
        pair_count,
        lane,
        mixed_from,
        w_in,
        species,
        species_gain,
        positions,
        cotangent,
    )
    gath = gathered(pack, "space")
    group = min(spaces, 8) * atoms
    messages, scaled = pl.pallas_call(
        functools.partial(main_kernel, spaces),
        out_shape=(
            jax.ShapeDtypeStruct((NHARM, channels, atoms), BF),
            jax.ShapeDtypeStruct((channels, atoms), BF),
        ),
        in_specs=[SMEM] + [VMEM] * 8,
        out_specs=(VMEM, VMEM),
        scratch_shapes=[
            pltpu.VMEM((NRAD, 3 * atoms, atoms), BF),
            pltpu.VMEM((2 * NHARM * channels, 3 * atoms), BF),
            pltpu.VMEM((3 * atoms, 8), F32),
            pltpu.VMEM((16, atoms), F32),
            pltpu.VMEM((NRAD, channels, atoms), F32),
            pltpu.VMEM((2 * NHARM, channels, atoms), F32),
            pltpu.VMEM(((2 * KLONG + 1) * rows, group), BF),
            pltpu.VMEM((2 * KMODE, group), BF),
        ],
        compiler_params=params,
        name="main",
    )(
        place,
        gath,
        cot_prev,
        cotangent,
        cot_next,
        wave_ints,
        w_rad,
        species,
        species_gain,
    )
    all_scaled = lax.all_gather(scaled, "chan", axis=0, tiled=True)
    grad_features = pl.pallas_call(
        final_kernel,
        out_shape=jax.ShapeDtypeStruct((channels, atoms), F32),
        in_specs=[SMEM, VMEM, VMEM],
        out_specs=VMEM,
        compiler_params=params,
        name="final",
    )(lane, w_in, all_scaled)
    return (messages, grad_features)


def solution(mesh):
    return jax.shard_map(
        on_device,
        mesh=mesh,
        in_specs=(
            P("chan", "space"),
            P(None, "space"),
            P("space"),
            P("space"),
            P("space"),
            P("space"),
            P("space"),
            P(),
            P(None, "chan"),
            P(),
            P(None, "chan"),
            P(None, "chan", "space"),
        ),
        out_specs=(P(None, "chan", "space"), P("chan", "space")),
        check_vma=False,
    )
```

```python
import functools
import math

import jax
import jax.numpy as jnp
from jax import lax
from jax.experimental import pallas as pl
from jax.experimental.pallas import tpu as pltpu
from jax.sharding import PartitionSpec as P

NSPEC = 6
BLOCK = 64
REACH = 4
NRAD = 16
NHARM = 9
KLONG = 8
KMODE = 128
MID = NRAD // 2

SLICE_WIDTH = 0.5
CUTOFF = SLICE_WIDTH * REACH
SIDE_WIDTH = 12.0
GAP_HEIGHT = 24.0
SIDE_CENTRE = 0.75
SCREEN = 0.5
HIGH = lax.Precision.HIGHEST
BF = jnp.bfloat16
F32 = jnp.float32
R3 = math.sqrt(3.0)
R5 = math.sqrt(5.0)
R15 = math.sqrt(15.0)

VMEM = pl.BlockSpec(memory_space=pltpu.VMEM)
SMEM = pl.BlockSpec(memory_space=pltpu.SMEM)


def dot_nt(a, b):
    return lax.dot_general(a, b, (((1,), (1,)), ((), ())), preferred_element_type=F32)


def dot_nn(a, b):
    return lax.dot_general(a, b, (((1,), (0,)), ((), ())), preferred_element_type=F32)


def harmonic_rows(x, y, z):
    s = x * x + y * y + z * z
    return [
        None,
        R3 * x,
        R3 * y,
        R3 * z,
        R15 * x * y,
        R15 * y * z,
        0.5 * R5 * (3.0 * z * z - s),
        R15 * x * z,
        0.5 * R15 * (x * x - y * y),
    ]


def shift_terms(x, y, z):
    q = R15 / R3
    return {
        (1, 0): -R3 * x,
        (2, 0): -R3 * y,
        (3, 0): -R3 * z,
        (4, 1): -q * y,
        (4, 2): -q * x,
        (4, 0): R15 * x * y,
        (5, 3): -q * y,
        (5, 2): -q * z,
        (5, 0): R15 * y * z,
        (6, 3): (-2.0 * R5 / R3) * z,
        (6, 1): (R5 / R3) * x,
        (6, 2): (R5 / R3) * y,
        (6, 0): 0.5 * R5 * (2.0 * z * z - x * x - y * y),
        (7, 3): -q * x,
        (7, 1): -q * z,
        (7, 0): R15 * x * z,
        (8, 1): -q * x,
        (8, 2): q * y,
        (8, 0): 0.5 * R15 * (x * x - y * y),
    }


def sincos_turns(turns):
    r = turns - jnp.floor(turns + 0.5)
    x = r * math.pi
    x2 = x * x
    s = jnp.full_like(x, -1.0 / math.factorial(11))
    for k, sign in ((9, 1.0), (7, -1.0), (5, 1.0), (3, -1.0), (1, 1.0)):
        s = s * x2 + sign / math.factorial(k)
    s = s * x
    c = jnp.full_like(x, 1.0 / math.factorial(12))
    for k, sign in ((10, -1.0), (8, 1.0), (6, -1.0), (4, 1.0), (2, -1.0), (0, 1.0)):
        c = c * x2 + sign / math.factorial(k)
    return 1.0 - 2.0 * s * s, 2.0 * s * c


def valid_row(count_ref, atoms):
    lane = lax.broadcasted_iota(jnp.int32, (1, atoms), 1)
    limit = jnp.zeros((1, atoms), jnp.int32)
    for b in range(atoms // BLOCK):
        limit = jnp.where(lane // BLOCK == b, count_ref[b] + b * BLOCK, limit)
    return (lane < limit).astype(F32)


def gain_rows(species_ref, species_gain_ref):
    ids = species_ref[...]
    rows = lax.broadcasted_iota(jnp.int32, (8, ids.shape[1]), 0)
    onehot = (rows == ids).astype(F32)[:NSPEC]
    return lax.dot_general(
        species_gain_ref[...],
        onehot,
        (((0,), (0,)), ((), ())),
        precision=HIGH,
        preferred_element_type=F32,
    )


def tail_rows(pos, flags, valid):
    atoms = pos.shape[1]
    top = pos.astype(BF).astype(F32)
    rest = pos - top
    mid = rest.astype(BF).astype(F32)
    low = rest - mid
    return jnp.concatenate([top, mid, low, flags, valid, jnp.zeros((5, atoms), F32)], 0).astype(BF)


def prep_kernel(
    live_ref,
    count_hbm,
    home_hbm,
    reach_hbm,
    pos_hbm,
    cot_hbm,
    species_hbm,
    gain_hbm,
    feats_hbm,
    w_hbm,
    halo_ref,
    gain_ref,
    feats_ref,
    w_ref,
    count_ref,
    home_ref,
    reach_ref,
    pos_ref,
    species_ref,
    species_gain_ref,
    sems,
):
    rows, atoms = cot_hbm.shape
    pairs = (
        (count_hbm, count_ref),
        (home_hbm, home_ref),
        (reach_hbm, reach_ref),
        (pos_hbm, pos_ref),
        (species_hbm, species_ref),
        (gain_hbm, species_gain_ref),
        (cot_hbm, halo_ref.at[0:rows, :]),
        (feats_hbm, feats_ref),
        (w_hbm, w_ref),
    )
    copies = [pltpu.make_async_copy(a, b, sems.at[i]) for i, (a, b) in enumerate(pairs)]
    for copy in copies:
        copy.start()
    for copy in copies[:6]:
        copy.wait()
    lane = lax.broadcasted_iota(jnp.int32, (1, atoms), 1)
    flags = jnp.zeros((1, atoms), F32)
    for p in range(home_ref.shape[0]):
        slot = home_ref[p] * REACH + reach_ref[p] - 1
        flags = jnp.where(jnp.logical_and(lane == slot, p < live_ref[0]), 1.0, flags)
    valid = valid_row(count_ref, atoms)
    halo_ref[rows:, :] = tail_rows(pos_ref[...], flags, valid)
    gain_ref[...] = gain_rows(species_ref, species_gain_ref) * valid
    for copy in copies[6:]:
        copy.wait()


def source_kernel(
    lane_ref, own_ref, first_ref, other_ref, w_ref, gain_ref, source_ref, all_ref, mix_ref
):
    channels, atoms = source_ref.shape
    lane = lane_ref[0]
    pieces = [own_ref[...], first_ref[...]]
    if other_ref is not None:
        pieces += [other_ref[m * channels : (m + 1) * channels, :] for m in range(2)]
    for m, piece in enumerate(pieces):
        at = pl.multiple_of((lane ^ m) * channels, channels)
        all_ref[pl.ds(at, channels), :] = piece
    mix_ref[...] = lax.dot_general(
        w_ref[...], all_ref[...], (((0,), (0,)), ((), ())), preferred_element_type=F32
    )
    mixed = mix_ref[pl.ds(pl.multiple_of(lane * channels, channels), channels), :]
    source_ref[...] = (mixed * gain_ref[...]).astype(BF)


def geometry(place, spaces, halos, cols_ref, live_ref, coord_ref):
    atoms = halos[0].shape[1]
    blocks = atoms // BLOCK
    length = SLICE_WIDTH * blocks * spaces
    even = lax.rem(place, 2) == 0
    wrap = jnp.where(place == 0, -length, jnp.where(place == spaces - 1, length, 0.0))
    centre = (place.astype(F32) + 0.5) * (SLICE_WIDTH * blocks)
    lane = lax.broadcasted_iota(jnp.int32, (1, atoms), 1)
    home = lane // BLOCK
    tails = [h[h.shape[0] - 16 :, :] for h in halos]

    def flag_row(tail, h, r):
        index = h * REACH + r - 1
        return jnp.broadcast_to(tail[9:10, index : index + 1].astype(F32), (1, atoms))

    coords, valids = [], []
    for t in range(3):
        x, y, z = unpack_pos(tails[t])
        x = x - (centre - wrap) if t == 2 else x - centre
        x = x * (1.0 / CUTOFF)
        y = (y - SIDE_CENTRE) * (1.0 / CUTOFF)
        z = (z - SIDE_CENTRE) * (1.0 / CUTOFF)
        coords.append((x, y, z))
        valids.append(tails[t][10:11].astype(F32))
        padded = jnp.concatenate([x, y, z, valids[t], jnp.zeros((4, atoms), F32)], 0)
        coord_ref[t] = padded
        cols_ref[t * atoms : (t + 1) * atoms, :] = padded.T
    none = jnp.zeros((1, atoms), F32)
    for e in range(blocks):
        row = none
        for h in range(blocks):
            d = abs(e - h)
            value = none + 1.0 if d == 0 else flag_row(tails[0], min(e, h), d)
            row = jnp.where(home == h, value, row)
        live_ref[e : e + 1, :] = row
        ahead = none
        for h in range(blocks):
            d = e + blocks - h
            if d <= REACH:
                ahead = jnp.where(home == h, flag_row(tails[0], h, d), ahead)
        for t in (1, 2):
            behind = none
            for h in range(blocks):
                d = h + blocks - e
                if d <= REACH:
                    behind = jnp.where(home == h, flag_row(tails[t], e, d), behind)
            is_ahead = even if t == 1 else jnp.logical_not(even)
            live_ref[t * blocks + e : t * blocks + e + 1, :] = jnp.where(is_ahead, ahead, behind)
    return coords[0]


def radial_kernel(
    spaces,
    place_ref,
    own_ref,
    first_ref,
    second_ref,
    wave_ref,
    w_rad_ref,
    radial_ref,
    coord_ref,
    filt_ref,
    weight_ref,
    cols_ref,
    live_ref,
):
    atoms = own_ref.shape[1]
    length = SLICE_WIDTH * (atoms // BLOCK) * spaces
    halos = (own_ref, first_ref, second_ref)
    xa, ya, za = geometry(place_ref[0], spaces, halos, cols_ref, live_ref, coord_ref)
    w_cols = w_rad_ref[...].T
    for n in range(NRAD):
        filt_ref[n] = jnp.broadcast_to(w_cols[:, n : n + 1], filt_ref.shape[1:])
    chunk = BLOCK
    for index in range(3 * atoms // chunk):
        lo = index * chunk
        at = slice(lo, lo + chunk)
        col = cols_ref[at, :]
        dx = col[:, 0:1] - xa
        dy = col[:, 1:2] - ya
        dz = col[:, 2:3] - za
        s = jnp.minimum(dx * dx + dy * dy + dz * dz, 1.0)
        gap = 1.0 - s
        envelope = gap * gap * live_ref[index : index + 1, :]
        if lo < atoms:
            other = lax.broadcasted_iota(jnp.int32, (chunk, atoms), 0) + lo
            me = lax.broadcasted_iota(jnp.int32, (chunk, atoms), 1)
            envelope = jnp.where(other == me, 0.0, envelope)
        off = s - MID / (NRAD - 1)
        middle = envelope * jnp.exp(-0.5 * (NRAD - 1) ** 2 * (off * off))
        radial_ref[MID, at, :] = middle.astype(BF)
        grow = jnp.exp((NRAD - 1.0) * s)
        value = middle
        for n in range(MID, NRAD - 1):
            value = value * (grow * math.exp(-(2 * n + 1) / 2))
            radial_ref[n + 1, at, :] = value.astype(BF)
        shrink = jnp.exp((1.0 - NRAD) * s)
        value = middle
        for n in range(MID, 0, -1):
            value = value * (shrink * math.exp((2 * n - 1) / 2))
            radial_ref[n - 1, at, :] = value.astype(BF)
    weight_ref[...] = mode_weights(wave_ref, length, atoms * spaces)


def near_mix(left_ref, radial_ref, filt_ref, total_ref):
    for n in range(NRAD):
        part = dot_nn(left_ref[...], radial_ref[n]).reshape(total_ref.shape) * filt_ref[n][None]
        if n == 0:
            total_ref[...] = part
        else:
            total_ref[...] += part


def near_scratch(channels, atoms):
    return [
        pltpu.VMEM((NHARM * channels, 3 * atoms), BF),
        pltpu.VMEM((NHARM, channels, atoms), F32),
    ]


def coord_rows(coord_ref, t):
    tile = coord_ref[t]
    return (tile[0:1], tile[1:2], tile[2:3])


def near_grad_kernel(
    own_ref, first_ref, second_ref, radial_ref, coord_ref, filt_ref, grad_ref, left_ref, total_ref
):
    channels, atoms = grad_ref.shape
    for t, halo in enumerate((own_ref, first_ref, second_ref)):
        at = slice(t * atoms, (t + 1) * atoms)
        valid = coord_ref[t][3:4]
        grads = [
            halo[l * channels : (l + 1) * channels, :].astype(F32) * valid for l in range(NHARM)
        ]
        moved = list(grads)
        for (l, m), term in shift_terms(*coord_rows(coord_ref, t)).items():
            moved[m] = moved[m] + grads[l] * term
        for m in range(NHARM):
            left_ref[m * channels : (m + 1) * channels, at] = moved[m].astype(BF)
    near_mix(left_ref, radial_ref, filt_ref, total_ref)
    harm = harmonic_rows(*coord_rows(coord_ref, 0))
    grad = total_ref[0]
    for m in range(1, NHARM):
        grad = grad + total_ref[m] * harm[m]
    grad_ref[...] = grad


def fill_terms(data, cos, sin, terms_ref, at):
    channels = data.shape[0]
    terms_ref[0:channels, at] = data.astype(BF)
    for k in range(KLONG):
        lo = (1 + 2 * k) * channels
        terms_ref[lo : lo + channels, at] = (data * cos[k : k + 1]).astype(BF)
        terms_ref[lo + channels : lo + 2 * channels, at] = (data * sin[k : k + 1]).astype(BF)


def far_part(weight_ref, fill, step, pairs, channels, terms_ref, modes_ref, longs_ref):
    group_atoms = terms_ref.shape[1]
    group = min(pairs, pairs * group_atoms // modes_ref.shape[1])
    atoms = modes_ref.shape[1] // (2 * pairs)
    sums = None
    for base in range(0, pairs, group):
        lax.fori_loop(0, group // step, fill, base)
        at = slice(base * 2 * atoms, base * 2 * atoms + group_atoms)
        part = dot_nt(terms_ref[...], modes_ref[:, at])
        sums = part if sums is None else sums + part
    rows_re, rows_im = [], []
    for k in range(KLONG + 1):
        w = weight_ref[k : k + 1, :]
        if k == 0:
            real = sums[0:channels]
            cos, sin = real[:, :KMODE], real[:, KMODE:]
        else:
            lo = (2 * k - 1) * channels
            real, imag = sums[lo : lo + channels], sums[lo + channels : lo + 2 * channels]
            cos = real[:, :KMODE] - imag[:, KMODE:]
            sin = real[:, KMODE:] + imag[:, :KMODE]
        cos, sin = cos * w, sin * w
        rows_re.append(jnp.concatenate([cos, sin], 1))
        if k > 0:
            rows_im.append(jnp.concatenate([sin, -cos], 1))
    waves = jnp.concatenate(rows_re + rows_im, 0).astype(BF)
    back = dot_nn(waves, modes_ref[:, 0:atoms])
    cos, sin = longs_ref[0:8, 0:atoms], longs_ref[8:16, 0:atoms]
    far = back[0:channels]
    for k in range(KLONG):
        lo = (1 + k) * channels
        far = far + back[lo : lo + channels] * cos[k : k + 1]
        lo = (1 + KLONG + k) * channels
        far = far + back[lo : lo + channels] * sin[k : k + 1]
    return far


def far_scratch(channels, atoms, spaces):
    return [pltpu.VMEM(((2 * KLONG + 1) * channels, min(spaces, 8) * atoms), BF)]


def scaled_kernel(
    length,
    held_ref,
    near_ref,
    weight_ref,
    gain_ref,
    order_ref,
    scaled_ref,
    modes_ref,
    longs_ref,
    terms_ref,
):
    channels, atoms = near_ref.shape
    unit = channels + 16

    def fill(p, base):
        for q in range(2):
            tail = held_ref[base + p, q * unit + channels : (q + 1) * unit, :]
            first, second, third = phase_rows(*unpack_pos(tail), length)
            at = pl.ds(pl.multiple_of((2 * (base + p) + q) * atoms, atoms), atoms)
            modes_ref[:, at] = mode_table(second, third)
            longs_ref[0:8, at] = first[0]
            longs_ref[8:16, at] = first[1]
            cot = held_ref[base + p, q * unit : q * unit + channels, :].astype(F32)
            at = pl.ds(pl.multiple_of((2 * p + q) * atoms, atoms), atoms)
            fill_terms(cot * tail[10:11].astype(F32), *first, terms_ref, at)
        return base

    far = far_part(
        weight_ref, fill, 1, held_ref.shape[0], channels, terms_ref, modes_ref, longs_ref
    )
    scaled_ref[...] = ((near_ref[...] + far) * gain_ref[...]).astype(BF)


def near_messages_kernel(
    source_ref,
    first_ref,
    second_ref,
    radial_ref,
    coord_ref,
    filt_ref,
    scalar_ref,
    rest_ref,
    left_ref,
    total_ref,
):
    channels, atoms = source_ref.shape
    for t, ref in enumerate((source_ref, first_ref, second_ref)):
        at = slice(t * atoms, (t + 1) * atoms)
        left_ref[0:channels, at] = ref[...]
        source = ref[...].astype(F32)
        harm = harmonic_rows(*coord_rows(coord_ref, t))
        for m in range(1, NHARM):
            left_ref[m * channels : (m + 1) * channels, at] = (source * harm[m]).astype(BF)
    near_mix(left_ref, radial_ref, filt_ref, total_ref)
    valid = coord_ref[0][3:4]
    sums = [total_ref[m] for m in range(NHARM)]
    near = list(sums)
    for (l, m), term in shift_terms(*coord_rows(coord_ref, 0)).items():
        near[l] = near[l] + sums[m] * term
    scalar_ref[...] = near[0] * valid
    for l in range(1, NHARM):
        rest_ref[l - 1] = (near[l] * valid).astype(BF)


def messages_kernel(
    held_ref,
    held_two_ref,
    scalar_ref,
    rest_ref,
    coord_ref,
    weight_ref,
    modes_ref,
    longs_ref,
    messages_ref,
    token_ref,
    terms_ref,
):
    channels, atoms = scalar_ref.shape
    pairs = 2 * held_ref.shape[0]

    def fill(index, base):
        for r, ref in enumerate((held_ref, held_two_ref)):
            for q in range(2):
                data = ref[base // 2 + index, q * channels : (q + 1) * channels, :]
                m = 4 * index + 2 * r + q
                at = pl.ds(pl.multiple_of((2 * base + m) * atoms, atoms), atoms)
                cos, sin = longs_ref[0:8, at], longs_ref[8:16, at]
                at = pl.ds(pl.multiple_of(m * atoms, atoms), atoms)
                fill_terms(data.astype(F32), cos, sin, terms_ref, at)
        return base

    far = far_part(weight_ref, fill, 2, pairs, channels, terms_ref, modes_ref, longs_ref)
    valid = coord_ref[0][3:4]
    messages_ref[0] = (scalar_ref[...] + far * valid).astype(BF)
    messages_ref[1:NHARM] = rest_ref[...]
    token_ref[...] = jnp.zeros_like(token_ref)


def final_kernel(
    lane_ref, w_ref, own_ref, first_ref, other_ref, token_ref, out_ref, all_ref
):
    channels = out_ref.shape[0]
    lane = lane_ref[0]
    pieces = [own_ref[...], first_ref[...]]
    if other_ref is not None:
        pieces += [other_ref[m * channels : (m + 1) * channels, :] for m in range(2)]
    for m, piece in enumerate(pieces):
        at = pl.multiple_of((lane ^ m) * channels, channels)
        all_ref[pl.ds(at, channels), :] = piece
    first = pl.multiple_of(lane * channels, channels)
    out_ref[...] = dot_nn(w_ref[pl.ds(first, channels), :], all_ref[...])


def two_chan(kernel, place):
    def without(*refs):
        kernel(*refs[:place], None, *refs[place:])

    return without


def cost(micros):
    return pl.CostEstimate(
        flops=int(micros * 1e9), bytes_accessed=int(micros * 3e6), transcendentals=0
    )


def swapped(block, axis, bit):
    return lax.ppermute(block, axis, [(i, i ^ bit) for i in range(lax.axis_size(axis))])


def chan_pieces(raw, kept):
    first = swapped(raw, "chan", 1)
    if lax.axis_size("chan") == 2:
        return [kept, first]
    return [kept, first, swapped(jnp.concatenate([kept, first], 0), "chan", 2)]


def on_device(
    features,
    positions,
    species,
    block_count,
    pair_home,
    pair_reach,
    pair_count,
    wave_ints,
    species_gain,
    w_in,
    w_rad,
    cotangent,
):
    channels, atoms = features.shape
    spaces = lax.axis_size("space")
    chans = lax.axis_size("chan")
    length = SLICE_WIDTH * (atoms // BLOCK) * spaces
    place = lax.axis_index("space").astype(jnp.int32).reshape(1)
    lane = lax.axis_index("chan").astype(jnp.int32).reshape(1)
    rows = NHARM * channels + 16
    species = species.reshape(1, atoms)
    shape = jax.ShapeDtypeStruct

    def call(kernel, out_shape, smem, vmem, scratch, name, micros):
        return pl.pallas_call(
            kernel,
            out_shape=out_shape,
            in_specs=[SMEM] * len(smem) + [VMEM] * len(vmem),
            out_specs=jax.tree.map(lambda _: VMEM, out_shape),
            scratch_shapes=scratch,
            compiler_params=pltpu.CompilerParams(vmem_limit_bytes=32 * 1024 * 1024),
            cost_estimate=cost(micros),
            name=name,
        )(*smem, *vmem)

    def in_hbm(x):
        return pltpu.with_memory_space_constraint(x, pltpu.HBM)

    own, gain, feats_copy, w_copy = pl.pallas_call(
        prep_kernel,
        out_shape=(
            shape((rows, atoms), BF),
            shape((channels, atoms), F32),
            shape(features.shape, BF),
            shape(w_in.shape, BF),
        ),
        in_specs=[SMEM] + [pl.BlockSpec(memory_space=pltpu.HBM)] * 9,
        out_specs=(VMEM,) * 4,
        scratch_shapes=[
            pltpu.SMEM(block_count.shape, jnp.int32),
            pltpu.SMEM(pair_home.shape, jnp.int32),
            pltpu.SMEM(pair_reach.shape, jnp.int32),
            pltpu.VMEM(positions.shape, F32),
            pltpu.VMEM(species.shape, jnp.int32),
            pltpu.VMEM(species_gain.shape, F32),
            pltpu.SemaphoreType.DMA((9,)),
        ],
        compiler_params=pltpu.CompilerParams(vmem_limit_bytes=8 * 1024 * 1024),
        cost_estimate=cost(1),
        name="prep",
    )(
        pair_count,
        *[
            in_hbm(x)
            for x in (
                block_count,
                pair_home,
                pair_reach,
                positions,
                cotangent.reshape(NHARM * channels, atoms),
                species,
                species_gain,
                features,
                w_in,
            )
        ]
    )
    pieces = chan_pieces(features, feats_copy)
    first = swapped(own, "space", 1)
    other = [i - 1 if i % 2 == 0 else i + 1 for i in range(spaces)]
    second = lax.ppermute(own, "space", [(i, other[i] % spaces) for i in range(spaces)])
    source = call(
        source_kernel if chans > 2 else two_chan(source_kernel, 3),
        shape((channels, atoms), BF),
        (lane,),
        (*pieces, w_copy, gain),
        [pltpu.VMEM((w_in.shape[0], atoms), BF), pltpu.VMEM((w_in.shape[1], atoms), F32)],
        "source",
        1,
    )
    source_first = swapped(source, "space", 1)
    source_second = lax.ppermute(source, "space", [(i, other[i] % spaces) for i in range(spaces)])
    cut = NHARM * channels
    unit = 2 * (channels + 16)
    block = jnp.concatenate([own[:channels], own[cut:], first[:channels], first[cut:]], 0)
    held = jnp.concatenate([block[None], swapped(block, "space", 2)[None]], 0)
    sources = jnp.concatenate([source, source_first], 0)[None]
    bit = 4
    while bit < spaces:
        flat = jnp.concatenate(
            [held.reshape(-1, atoms), sources.reshape(-1, atoms)], 0
        )
        other_flat = swapped(flat, "space", bit)
        split = held.shape[0] * unit
        held = jnp.concatenate([held, other_flat[:split].reshape(held.shape)], 0)
        sources = jnp.concatenate([sources, other_flat[split:].reshape(sources.shape)], 0)
        bit *= 2
    sources_two = swapped(sources, "space", 2)
    radial, coord, filt, weight = call(
        functools.partial(radial_kernel, spaces),
        (
            shape((NRAD, 3 * atoms, atoms), BF),
            shape((3, 8, atoms), F32),
            shape((NRAD, channels, atoms), F32),
            shape((16, KMODE), F32),
        ),
        (place,),
        (own, first, second, wave_ints, w_rad),
        [pltpu.VMEM((3 * atoms, 8), F32), pltpu.VMEM((16, atoms), F32)],
        "radial",
        3,
    )
    near_grad = call(
        near_grad_kernel,
        shape((channels, atoms), F32),
        (),
        (own, first, second, radial, coord, filt),
        near_scratch(channels, atoms),
        "near_grad",
        3,
    )
    scalar, rest = call(
        near_messages_kernel,
        (shape((channels, atoms), F32), shape((NHARM - 1, channels, atoms), BF)),
        (),
        (source, source_first, source_second, radial, coord, filt),
        near_scratch(channels, atoms),
        "near_messages",
        3,
    )
    scaled, modes, longs = call(
        functools.partial(scaled_kernel, length),
        (
            shape((channels, atoms), BF),
            shape((2 * KMODE, spaces * atoms), BF),
            shape((16, spaces * atoms), F32),
        ),
        (),
        (held, near_grad, weight, gain, scalar),
        far_scratch(channels, atoms, spaces),
        "scaled",
        2,
    )
    scaled_pieces = chan_pieces(scaled, scaled)
    messages, token = call(
        messages_kernel,
        (shape((NHARM, channels, atoms), BF), shape((8, 128), F32)),
        (),
        (sources, sources_two, scalar, rest, coord, weight, modes, longs),
        far_scratch(channels, atoms, spaces),
        "messages",
        2,
    )
    grad_features = call(
        final_kernel if chans > 2 else two_chan(final_kernel, 4),
        shape((channels, atoms), F32),
        (lane,),
        (w_copy, *scaled_pieces, token),
        [pltpu.VMEM((chans * channels, atoms), BF)],
        "final",
        1,
    )
    return (messages, grad_features)


def mode_weights(wave_ref, length, total):
    k = wave_ref[...]
    count = k.shape[1]
    k = jnp.where(k[0:1] < 0, -k, k)
    k1, k2, k3 = k[0:1], k[1:2], k[2:3]
    code = jnp.where(k3 == 4, 76 + k2, (k2 + 4) * 8 + k3 + 4)
    rows = lax.broadcasted_iota(jnp.int32, (KMODE, count), 0)
    hot = (rows == code).astype(F32).astype(BF)
    longs = lax.broadcasted_iota(jnp.int32, (16, count), 0)
    hot1 = (longs == k1).astype(F32).astype(BF)
    mult = dot_nt(hot1, hot)
    lane = lax.broadcasted_iota(jnp.int32, (16, KMODE), 1)
    row = lax.broadcasted_iota(jnp.int32, (16, KMODE), 0)
    g2 = jnp.where(lane < 72, lane // 8 - 4, lane - 76).astype(F32)
    g3 = jnp.where(lane < 72, lane % 8 - 4, 4).astype(F32)
    f1 = row.astype(F32) * (2.0 * math.pi / length)
    f2 = g2 * (2.0 * math.pi / SIDE_WIDTH)
    f3 = g3 * (2.0 * math.pi / GAP_HEIGHT)
    ksq = f1 * f1 + f2 * f2 + f3 * f3
    value = jnp.exp(-0.5 * ksq) / (ksq + SCREEN * SCREEN) * (1.0 / math.sqrt(count * total))
    return jnp.where(mult > 0.0, mult * value, 0.0)


def phase_rows(x, y, z, length):
    atoms = x.shape[1]
    step = lax.broadcasted_iota(jnp.int32, (8, atoms), 0).astype(F32)
    first = sincos_turns((step + 1.0) * (x * (1.0 / length)))
    second = sincos_turns((step - 4.0) * (y * (1.0 / SIDE_WIDTH)))
    third = sincos_turns((step - 4.0) * (z * (1.0 / GAP_HEIGHT)))
    return first, second, third


def mode_table(second, third):
    c2, s2 = second
    c3, s3 = third
    atoms = c2.shape[1]
    cos, sin = [], []
    for k2 in range(9):
        a = c2[k2 : k2 + 1] if k2 < 8 else c2[0:1]
        b = s2[k2 : k2 + 1] if k2 < 8 else -s2[0:1]
        cos.append(a * c3 - b * s3)
        sin.append(a * s3 + b * c3)
    a, b = c3[0:1], -s3[0:1]
    cos.append(c2 * a - s2 * b)
    sin.append(c2 * b + s2 * a)
    one = lax.broadcasted_iota(jnp.int32, (8, atoms), 0) == 0
    cos.append(jnp.where(one, c2[0:1] * a + s2[0:1] * b, 0.0))
    sin.append(jnp.where(one, c2[0:1] * b - s2[0:1] * a, 0.0))
    pad = jnp.zeros((KMODE - 88, atoms), F32)
    return jnp.concatenate(cos + [pad] + sin + [pad], 0).astype(BF)


def unpack_pos(tail):
    t = tail.astype(F32)
    pos = (t[0:3] + t[3:6]) + t[6:9]
    return pos[0:1], pos[1:2], pos[2:3]


def solution(mesh):
    return jax.shard_map(
        on_device,
        mesh=mesh,
        in_specs=(
            P("chan", "space"),
            P(None, "space"),
            P("space"),
            P("space"),
            P("space"),
            P("space"),
            P("space"),
            P(),
            P(None, "chan"),
            P(),
            P(None, "chan"),
            P(None, "chan", "space"),
        ),
        out_specs=(P(None, "chan", "space"), P("chan", "space")),
        check_vma=False,
    )
```

```python
import functools
import math

import jax
import jax.numpy as jnp
from jax import lax
from jax.experimental import pallas as pl
from jax.experimental.pallas import tpu as pltpu
from jax.sharding import PartitionSpec as P

NSPEC = 6
BLOCK = 64
REACH = 4
NRAD = 16
NHARM = 9
KLONG = 8
KMODE = 128
MID = NRAD // 2

SLICE_WIDTH = 0.5
CUTOFF = SLICE_WIDTH * REACH
SIDE_WIDTH = 12.0
GAP_HEIGHT = 24.0
SIDE_CENTRE = 0.75
SCREEN = 0.5
HIGH = lax.Precision.HIGHEST
BF = jnp.bfloat16
F32 = jnp.float32
R3 = math.sqrt(3.0)
R5 = math.sqrt(5.0)
R15 = math.sqrt(15.0)

COST = dict(prep=1, source=1, radial=3, near_grad=3, near_messages=1.5, scaled=2, half=0.2, messages=2, final=1)
VMEM = pl.BlockSpec(memory_space=pltpu.VMEM)
SMEM = pl.BlockSpec(memory_space=pltpu.SMEM)


def dot_nt(a, b):
    return lax.dot_general(a, b, (((1,), (1,)), ((), ())), preferred_element_type=F32)


def dot_nn(a, b):
    return lax.dot_general(a, b, (((1,), (0,)), ((), ())), preferred_element_type=F32)


def harmonic_rows(x, y, z):
    s = x * x + y * y + z * z
    return [
        None,
        R3 * x,
        R3 * y,
        R3 * z,
        R15 * x * y,
        R15 * y * z,
        0.5 * R5 * (3.0 * z * z - s),
        R15 * x * z,
        0.5 * R15 * (x * x - y * y),
    ]


def shift_terms(x, y, z):
    q = R15 / R3
    return {
        (1, 0): -R3 * x,
        (2, 0): -R3 * y,
        (3, 0): -R3 * z,
        (4, 1): -q * y,
        (4, 2): -q * x,
        (4, 0): R15 * x * y,
        (5, 3): -q * y,
        (5, 2): -q * z,
        (5, 0): R15 * y * z,
        (6, 3): (-2.0 * R5 / R3) * z,
        (6, 1): (R5 / R3) * x,
        (6, 2): (R5 / R3) * y,
        (6, 0): 0.5 * R5 * (2.0 * z * z - x * x - y * y),
        (7, 3): -q * x,
        (7, 1): -q * z,
        (7, 0): R15 * x * z,
        (8, 1): -q * x,
        (8, 2): q * y,
        (8, 0): 0.5 * R15 * (x * x - y * y),
    }


def sincos_turns(turns):
    r = turns - jnp.floor(turns + 0.5)
    x = r * math.pi
    x2 = x * x
    s = jnp.full_like(x, -1.0 / math.factorial(11))
    for k, sign in ((9, 1.0), (7, -1.0), (5, 1.0), (3, -1.0), (1, 1.0)):
        s = s * x2 + sign / math.factorial(k)
    s = s * x
    c = jnp.full_like(x, 1.0 / math.factorial(12))
    for k, sign in ((10, -1.0), (8, 1.0), (6, -1.0), (4, 1.0), (2, -1.0), (0, 1.0)):
        c = c * x2 + sign / math.factorial(k)
    return 1.0 - 2.0 * s * s, 2.0 * s * c


def valid_row(count_ref, atoms):
    lane = lax.broadcasted_iota(jnp.int32, (1, atoms), 1)
    limit = jnp.zeros((1, atoms), jnp.int32)
    for b in range(atoms // BLOCK):
        limit = jnp.where(lane // BLOCK == b, count_ref[b] + b * BLOCK, limit)
    return (lane < limit).astype(F32)


def gain_rows(species_ref, species_gain_ref):
    ids = species_ref[...]
    rows = lax.broadcasted_iota(jnp.int32, (8, ids.shape[1]), 0)
    onehot = (rows == ids).astype(F32)[:NSPEC]
    return lax.dot_general(
        species_gain_ref[...],
        onehot,
        (((0,), (0,)), ((), ())),
        precision=HIGH,
        preferred_element_type=F32,
    )


def tail_rows(pos, flags, valid):
    atoms = pos.shape[1]
    top = pos.astype(BF).astype(F32)
    rest = pos - top
    mid = rest.astype(BF).astype(F32)
    low = rest - mid
    return jnp.concatenate([top, mid, low, flags, valid, jnp.zeros((5, atoms), F32)], 0).astype(BF)


def prep_kernel(
    live_ref,
    count_hbm,
    home_hbm,
    reach_hbm,
    pos_hbm,
    cot_hbm,
    species_hbm,
    gain_hbm,
    feats_hbm,
    w_hbm,
    head_ref,
    gain_ref,
    feats_ref,
    w_ref,
    count_ref,
    home_ref,
    reach_ref,
    pos_ref,
    species_ref,
    species_gain_ref,
    sems,
):
    channels, atoms = feats_hbm.shape
    pairs = (
        (count_hbm, count_ref),
        (home_hbm, home_ref),
        (reach_hbm, reach_ref),
        (pos_hbm, pos_ref),
        (species_hbm, species_ref),
        (gain_hbm, species_gain_ref),
        (cot_hbm.at[0:channels, :], head_ref.at[0:channels, :]),
        (feats_hbm, feats_ref),
        (w_hbm, w_ref),
    )
    copies = [pltpu.make_async_copy(a, b, sems.at[i]) for i, (a, b) in enumerate(pairs)]
    for copy in copies:
        copy.start()
    for copy in copies[:6]:
        copy.wait()
    lane = lax.broadcasted_iota(jnp.int32, (1, atoms), 1)
    flags = jnp.zeros((1, atoms), F32)
    for p in range(home_ref.shape[0]):
        slot = home_ref[p] * REACH + reach_ref[p] - 1
        flags = jnp.where(jnp.logical_and(lane == slot, p < live_ref[0]), 1.0, flags)
    valid = valid_row(count_ref, atoms)
    head_ref[channels:, :] = tail_rows(pos_ref[...], flags, valid)
    gain_ref[...] = gain_rows(species_ref, species_gain_ref) * valid
    for copy in copies[6:]:
        copy.wait()


def source_kernel(chans, lane_ref, *refs):
    pieces, (w_ref, gain_ref, head_ref) = refs[:chans], refs[chans : chans + 3]
    out_ref, all_ref, mix_ref = refs[-3:]
    channels = gain_ref.shape[0]
    lane = lane_ref[0]
    out_ref[0 : channels + 16, :] = head_ref[...]
    for m, piece in enumerate(pieces):
        at = pl.multiple_of((lane ^ m) * channels, channels)
        all_ref[pl.ds(at, channels), :] = piece[...]
    mix_ref[...] = lax.dot_general(
        w_ref[...], all_ref[...], (((0,), (0,)), ((), ())), preferred_element_type=F32
    )
    mixed = mix_ref[pl.ds(pl.multiple_of(lane * channels, channels), channels), :]
    out_ref[channels + 16 :, :] = (mixed * gain_ref[...]).astype(BF)


def geometry(place, spaces, halos, channels, cols_ref, live_ref, coord_ref):
    atoms = halos[0].shape[1]
    blocks = atoms // BLOCK
    length = SLICE_WIDTH * blocks * spaces
    even = lax.rem(place, 2) == 0
    wrap = jnp.where(place == 0, -length, jnp.where(place == spaces - 1, length, 0.0))
    centre = (place.astype(F32) + 0.5) * (SLICE_WIDTH * blocks)
    lane = lax.broadcasted_iota(jnp.int32, (1, atoms), 1)
    home = lane // BLOCK
    tails = []
    for h in halos:
        cut = h.shape[0] - channels
        tails.append(h[cut - 16 : cut, :])

    def flag_row(tail, h, r):
        index = h * REACH + r - 1
        return jnp.broadcast_to(tail[9:10, index : index + 1].astype(F32), (1, atoms))

    coords, valids = [], []
    for t in range(3):
        x, y, z = unpack_pos(tails[t])
        x = x - (centre - wrap) if t == 2 else x - centre
        x = x * (1.0 / CUTOFF)
        y = (y - SIDE_CENTRE) * (1.0 / CUTOFF)
        z = (z - SIDE_CENTRE) * (1.0 / CUTOFF)
        coords.append((x, y, z))
        valids.append(tails[t][10:11].astype(F32))
        padded = jnp.concatenate([x, y, z, valids[t], jnp.zeros((4, atoms), F32)], 0)
        coord_ref[t] = padded
        cols_ref[t * atoms : (t + 1) * atoms, :] = padded.T
    none = jnp.zeros((1, atoms), F32)
    for e in range(blocks):
        row = none
        for h in range(blocks):
            d = abs(e - h)
            value = none + 1.0 if d == 0 else flag_row(tails[0], min(e, h), d)
            row = jnp.where(home == h, value, row)
        live_ref[e : e + 1, :] = row
        ahead = none
        for h in range(blocks):
            d = e + blocks - h
            if d <= REACH:
                ahead = jnp.where(home == h, flag_row(tails[0], h, d), ahead)
        for t in (1, 2):
            behind = none
            for h in range(blocks):
                d = h + blocks - e
                if d <= REACH:
                    behind = jnp.where(home == h, flag_row(tails[t], e, d), behind)
            is_ahead = even if t == 1 else jnp.logical_not(even)
            live_ref[t * blocks + e : t * blocks + e + 1, :] = jnp.where(is_ahead, ahead, behind)
    return coords[0]


def radial_kernel(
    spaces,
    place_ref,
    own_ref,
    first_ref,
    second_ref,
    wave_ref,
    w_rad_ref,
    radial_ref,
    coord_ref,
    filt_ref,
    weight_ref,
    cols_ref,
    live_ref,
):
    atoms = own_ref.shape[1]
    length = SLICE_WIDTH * (atoms // BLOCK) * spaces
    halos = (own_ref, first_ref, second_ref)
    xa, ya, za = geometry(
        place_ref[0], spaces, halos, w_rad_ref.shape[1], cols_ref, live_ref, coord_ref
    )
    w_cols = w_rad_ref[...].T
    for n in range(NRAD):
        filt_ref[n] = jnp.broadcast_to(w_cols[:, n : n + 1], filt_ref.shape[1:])
    chunk = BLOCK
    for index in range(3 * atoms // chunk):
        lo = index * chunk
        at = slice(lo, lo + chunk)
        col = cols_ref[at, :]
        dx = col[:, 0:1] - xa
        dy = col[:, 1:2] - ya
        dz = col[:, 2:3] - za
        s = jnp.minimum(dx * dx + dy * dy + dz * dz, 1.0)
        gap = 1.0 - s
        envelope = gap * gap * live_ref[index : index + 1, :]
        if lo < atoms:
            other = lax.broadcasted_iota(jnp.int32, (chunk, atoms), 0) + lo
            me = lax.broadcasted_iota(jnp.int32, (chunk, atoms), 1)
            envelope = jnp.where(other == me, 0.0, envelope)
        off = s - MID / (NRAD - 1)
        middle = envelope * jnp.exp(-0.5 * (NRAD - 1) ** 2 * (off * off))
        radial_ref[MID, at, :] = middle.astype(BF)
        grow = jnp.exp((NRAD - 1.0) * s)
        value = middle
        for n in range(MID, NRAD - 1):
            value = value * (grow * math.exp(-(2 * n + 1) / 2))
            radial_ref[n + 1, at, :] = value.astype(BF)
        shrink = jnp.exp((1.0 - NRAD) * s)
        value = middle
        for n in range(MID, 0, -1):
            value = value * (shrink * math.exp((2 * n - 1) / 2))
            radial_ref[n - 1, at, :] = value.astype(BF)
    weight_ref[...] = mode_weights(wave_ref, length, atoms * spaces)


def near_mix(left_ref, radial_ref, filt_ref, total_ref):
    for n in range(NRAD):
        part = dot_nn(left_ref[...], radial_ref[n]).reshape(total_ref.shape) * filt_ref[n][None]
        if n == 0:
            total_ref[...] = part
        else:
            total_ref[...] += part


def near_scratch(channels, atoms):
    return [
        pltpu.VMEM((NHARM * channels, 3 * atoms), BF),
        pltpu.VMEM((NHARM, channels, atoms), F32),
    ]


def coord_rows(coord_ref, t):
    tile = coord_ref[t]
    return (tile[0:1], tile[1:2], tile[2:3])


def near_grad_kernel(
    own_ref, first_ref, second_ref, radial_ref, coord_ref, filt_ref, grad_ref, left_ref, total_ref
):
    channels, atoms = grad_ref.shape
    for t, halo in enumerate((own_ref, first_ref, second_ref)):
        at = slice(t * atoms, (t + 1) * atoms)
        valid = coord_ref[t][3:4]
        grads = [
            halo[l * channels : (l + 1) * channels, :].astype(F32) * valid for l in range(NHARM)
        ]
        moved = list(grads)
        for (l, m), term in shift_terms(*coord_rows(coord_ref, t)).items():
            moved[m] = moved[m] + grads[l] * term
        for m in range(NHARM):
            left_ref[m * channels : (m + 1) * channels, at] = moved[m].astype(BF)
    near_mix(left_ref, radial_ref, filt_ref, total_ref)
    harm = harmonic_rows(*coord_rows(coord_ref, 0))
    grad = total_ref[0]
    for m in range(1, NHARM):
        grad = grad + total_ref[m] * harm[m]
    grad_ref[...] = grad


def fill_terms(data, cos, sin, terms_ref, at):
    channels = data.shape[0]
    terms_ref[0:channels, at] = data.astype(BF)
    for k in range(KLONG):
        lo = (1 + 2 * k) * channels
        terms_ref[lo : lo + channels, at] = (data * cos[k : k + 1]).astype(BF)
        terms_ref[lo + channels : lo + 2 * channels, at] = (data * sin[k : k + 1]).astype(BF)


def gathered_sums(fill, pairs, terms_ref, modes_ref):
    span = terms_ref.shape[1]
    group = pairs * span // modes_ref.shape[1]
    sums = None
    for base in range(0, pairs, group):
        lax.fori_loop(0, group, fill, base)
        at = slice(base // group * span, (base // group + 1) * span)
        part = dot_nt(terms_ref[...], modes_ref[:, at])
        sums = part if sums is None else sums + part
    return sums


def far_field(sums, weight_ref, own_ref, own_longs_ref, channels):
    rows_re, rows_im = [], []
    for k in range(KLONG + 1):
        w = weight_ref[k : k + 1, :]
        if k == 0:
            real = sums[0:channels]
            cos, sin = real[:, :KMODE], real[:, KMODE:]
        else:
            lo = (2 * k - 1) * channels
            real, imag = sums[lo : lo + channels], sums[lo + channels : lo + 2 * channels]
            cos = real[:, :KMODE] - imag[:, KMODE:]
            sin = real[:, KMODE:] + imag[:, :KMODE]
        cos, sin = cos * w, sin * w
        rows_re.append(jnp.concatenate([cos, sin], 1))
        if k > 0:
            rows_im.append(jnp.concatenate([sin, -cos], 1))
    waves = jnp.concatenate(rows_re + rows_im, 0).astype(BF)
    back = dot_nn(waves, own_ref[...])
    cos, sin = own_longs_ref[0:8, :], own_longs_ref[8:16, :]
    far = back[0:channels]
    for k in range(KLONG):
        lo = (1 + k) * channels
        far = far + back[lo : lo + channels] * cos[k : k + 1]
        lo = (1 + KLONG + k) * channels
        far = far + back[lo : lo + channels] * sin[k : k + 1]
    return far


def far_scratch(channels, atoms, spaces):
    return [pltpu.VMEM(((2 * KLONG + 1) * channels, min(spaces // 2, 8) * atoms), BF)]


def cot_filler(length, held_ref, channels, modes_ref, longs_ref, terms_ref):
    unit = 2 * channels + 16
    atoms = held_ref.shape[2]

    def fill(p, base):
        for q in range(2):
            lo = q * unit
            tail = held_ref[base + p, lo + channels : lo + channels + 16, :]
            first, second, third = phase_rows(*unpack_pos(tail), length)
            at = pl.ds(pl.multiple_of((2 * (base + p) + q) * atoms, atoms), atoms)
            modes_ref[:, at] = mode_table(second, third)
            longs_ref[0:8, at] = first[0]
            longs_ref[8:16, at] = first[1]
            cot = held_ref[base + p, lo : lo + channels, :].astype(F32)
            at = pl.ds(pl.multiple_of((2 * p + q) * atoms, atoms), atoms)
            fill_terms(cot * tail[10:11].astype(F32), *first, terms_ref, at)
        return base

    return fill


def source_filler(held_ref, channels, longs_ref, terms_ref):
    unit = 2 * channels + 16
    atoms = held_ref.shape[2]

    def fill(p, base):
        for q in range(2):
            lo = q * unit + channels + 16
            data = held_ref[base + p, lo : lo + channels, :].astype(F32)
            at = pl.ds(pl.multiple_of((2 * (base + p) + q) * atoms, atoms), atoms)
            cos, sin = longs_ref[0:8, at], longs_ref[8:16, at]
            at = pl.ds(pl.multiple_of((2 * p + q) * atoms, atoms), atoms)
            fill_terms(data, cos, sin, terms_ref, at)
        return base

    return fill


def half_kernel(
    length,
    held_ref,
    cot_sums_ref,
    source_sums_ref,
    own_ref,
    own_longs_ref,
    terms_ref,
    modes_ref,
    longs_ref,
):
    pairs, rows, atoms = held_ref.shape
    channels = (rows // 2 - 16) // 2
    fill = cot_filler(length, held_ref, channels, modes_ref, longs_ref, terms_ref)
    cot_sums_ref[...] = gathered_sums(fill, pairs, terms_ref, modes_ref)
    fill = source_filler(held_ref, channels, longs_ref, terms_ref)
    source_sums_ref[...] = gathered_sums(fill, pairs, terms_ref, modes_ref)
    own_ref[...] = modes_ref[:, 0:atoms]
    own_longs_ref[...] = longs_ref[:, 0:atoms]


def scaled_kernel(
    length,
    rest_ref,
    near_ref,
    weight_ref,
    gain_ref,
    sums_ref,
    own_ref,
    own_longs_ref,
    order_ref,
    scaled_ref,
    modes_ref,
    longs_ref,
    terms_ref,
):
    channels = near_ref.shape[0]
    fill = cot_filler(length, rest_ref, channels, modes_ref, longs_ref, terms_ref)
    sums = gathered_sums(fill, rest_ref.shape[0], terms_ref, modes_ref) + sums_ref[...]
    far = far_field(sums, weight_ref, own_ref, own_longs_ref, channels)
    scaled_ref[...] = ((near_ref[...] + far) * gain_ref[...]).astype(BF)


def near_messages_kernel(
    own_ref,
    first_ref,
    second_ref,
    radial_ref,
    coord_ref,
    filt_ref,
    scalar_ref,
    rest_ref,
    left_ref,
    total_ref,
):
    channels, atoms = scalar_ref.shape
    for t, ref in enumerate((own_ref, first_ref, second_ref)):
        lo = ref.shape[0] - channels
        at = slice(t * atoms, (t + 1) * atoms)
        left_ref[0:channels, at] = ref[lo : lo + channels, :]
        source = ref[lo : lo + channels, :].astype(F32)
        harm = harmonic_rows(*coord_rows(coord_ref, t))
        for m in range(1, NHARM):
            left_ref[m * channels : (m + 1) * channels, at] = (source * harm[m]).astype(BF)
    near_mix(left_ref, radial_ref, filt_ref, total_ref)
    valid = coord_ref[0][3:4]
    sums = [total_ref[m] for m in range(NHARM)]
    near = list(sums)
    for (l, m), term in shift_terms(*coord_rows(coord_ref, 0)).items():
        near[l] = near[l] + sums[m] * term
    scalar_ref[...] = near[0] * valid
    for l in range(1, NHARM):
        rest_ref[l - 1] = (near[l] * valid).astype(BF)


def messages_kernel(
    held_ref,
    scalar_ref,
    rest_ref,
    coord_ref,
    weight_ref,
    sums_ref,
    own_ref,
    own_longs_ref,
    modes_ref,
    longs_ref,
    messages_ref,
    token_ref,
    terms_ref,
):
    channels = scalar_ref.shape[0]
    fill = source_filler(held_ref, channels, longs_ref, terms_ref)
    sums = gathered_sums(fill, held_ref.shape[0], terms_ref, modes_ref) + sums_ref[...]
    far = far_field(sums, weight_ref, own_ref, own_longs_ref, channels)
    valid = coord_ref[0][3:4]
    messages_ref[0] = (scalar_ref[...] + far * valid).astype(BF)
    messages_ref[1:NHARM] = rest_ref[...]
    token_ref[...] = jnp.zeros_like(token_ref)


def final_kernel(
    lane_ref, w_ref, own_ref, first_ref, other_ref, token_ref, out_ref, all_ref
):
    channels = out_ref.shape[0]
    lane = lane_ref[0]
    pieces = [own_ref[...], first_ref[...]]
    if other_ref is not None:
        pieces += [other_ref[m * channels : (m + 1) * channels, :] for m in range(2)]
    for m, piece in enumerate(pieces):
        at = pl.multiple_of((lane ^ m) * channels, channels)
        all_ref[pl.ds(at, channels), :] = piece
    first = pl.multiple_of(lane * channels, channels)
    out_ref[...] = dot_nn(w_ref[pl.ds(first, channels), :], all_ref[...])


def two_chan(kernel, place):
    def without(*refs):
        kernel(*refs[:place], None, *refs[place:])

    return without


def cost(micros):
    return pl.CostEstimate(
        flops=int(micros * 1e9), bytes_accessed=int(micros * 3e6), transcendentals=0
    )


def swapped(block, axis, bit):
    return lax.ppermute(block, axis, [(i, i ^ bit) for i in range(lax.axis_size(axis))])


def chan_pieces(raw, kept):
    first = swapped(raw, "chan", 1)
    if lax.axis_size("chan") == 2:
        return [kept, first]
    return [kept, first, swapped(jnp.concatenate([kept, first], 0), "chan", 2)]


def on_device(
    features,
    positions,
    species,
    block_count,
    pair_home,
    pair_reach,
    pair_count,
    wave_ints,
    species_gain,
    w_in,
    w_rad,
    cotangent,
):
    channels, atoms = features.shape
    spaces = lax.axis_size("space")
    chans = lax.axis_size("chan")
    length = SLICE_WIDTH * (atoms // BLOCK) * spaces
    place = lax.axis_index("space").astype(jnp.int32).reshape(1)
    lane = lax.axis_index("chan").astype(jnp.int32).reshape(1)
    species = species.reshape(1, atoms)
    shape = jax.ShapeDtypeStruct

    def call(kernel, out_shape, smem, vmem, scratch, name, micros):
        return pl.pallas_call(
            kernel,
            out_shape=out_shape,
            in_specs=[SMEM] * len(smem) + [VMEM] * len(vmem),
            out_specs=jax.tree.map(lambda _: VMEM, out_shape),
            scratch_shapes=scratch,
            compiler_params=pltpu.CompilerParams(vmem_limit_bytes=32 * 1024 * 1024),
            cost_estimate=cost(micros),
            name=name,
        )(*smem, *vmem)

    def in_hbm(x):
        return pltpu.with_memory_space_constraint(x, pltpu.HBM)

    cots = cotangent.reshape(NHARM * channels, atoms)
    head, gain, feats_copy, w_copy = pl.pallas_call(
        prep_kernel,
        out_shape=(
            shape((channels + 16, atoms), BF),
            shape((channels, atoms), F32),
            shape(features.shape, BF),
            shape(w_in.shape, BF),
        ),
        in_specs=[SMEM] + [pl.BlockSpec(memory_space=pltpu.HBM)] * 9,
        out_specs=(VMEM,) * 4,
        scratch_shapes=[
            pltpu.SMEM(block_count.shape, jnp.int32),
            pltpu.SMEM(pair_home.shape, jnp.int32),
            pltpu.SMEM(pair_reach.shape, jnp.int32),
            pltpu.VMEM(positions.shape, F32),
            pltpu.VMEM(species.shape, jnp.int32),
            pltpu.VMEM(species_gain.shape, F32),
            pltpu.SemaphoreType.DMA((9,)),
        ],
        compiler_params=pltpu.CompilerParams(vmem_limit_bytes=8 * 1024 * 1024),
        cost_estimate=cost(COST["prep"]),
        name="prep",
    )(
        pair_count,
        *[
            in_hbm(x)
            for x in (
                block_count,
                pair_home,
                pair_reach,
                positions,
                cots,
                species,
                species_gain,
                features,
                w_in,
            )
        ]
    )
    pieces = [feats_copy] + [swapped(features, "chan", m) for m in range(1, chans)]
    other = [i - 1 if i % 2 == 0 else i + 1 for i in range(spaces)]
    route = [(i, other[i] % spaces) for i in range(spaces)]
    second = lax.ppermute(cots, "space", route)
    first = swapped(cots, "space", 1)
    unit = call(
        functools.partial(source_kernel, chans),
        shape((2 * channels + 16, atoms), BF),
        (lane,),
        (*pieces, w_copy, gain, head, first, second),
        [pltpu.VMEM((w_in.shape[0], atoms), BF), pltpu.VMEM((w_in.shape[1], atoms), F32)],
        "source",
        COST["source"],
    )
    unit_first = swapped(unit, "space", 1)
    unit_second = lax.ppermute(unit[channels:], "space", route)
    block = jnp.concatenate([unit, unit_first], 0)
    held = block[None]
    bit = spaces // 2
    while bit > 2:
        held = jnp.concatenate([held, swapped(held, "space", bit)], 0)
        bit //= 2
    held_rest = swapped(held, "space", 2)
    radial, coord, filt, weight = call(
        functools.partial(radial_kernel, spaces),
        (
            shape((NRAD, 3 * atoms, atoms), BF),
            shape((3, 8, atoms), F32),
            shape((NRAD, channels, atoms), F32),
            shape((16, KMODE), F32),
        ),
        (place,),
        (unit, unit_first, unit_second, wave_ints, w_rad),
        [pltpu.VMEM((3 * atoms, 8), F32), pltpu.VMEM((16, atoms), F32)],
        "radial",
        COST["radial"],
    )
    near_grad = call(
        near_grad_kernel,
        shape((channels, atoms), F32),
        (),
        (cots, first, second, radial, coord, filt),
        near_scratch(channels, atoms),
        "near_grad",
        COST["near_grad"],
    )
    scalar, rest = call(
        near_messages_kernel,
        (shape((channels, atoms), F32), shape((NHARM - 1, channels, atoms), BF)),
        (),
        (unit, unit_first, unit_second, radial, coord, filt),
        near_scratch(channels, atoms),
        "near_messages",
        COST["near_messages"],
    )
    terms = ((2 * KLONG + 1) * channels, 2 * KMODE)
    table = pltpu.VMEM((2 * KMODE, spaces // 2 * atoms), BF)
    long_rows = pltpu.VMEM((16, spaces // 2 * atoms), F32)
    cot_sums, source_sums, modes_own, longs_own = call(
        functools.partial(half_kernel, length),
        (
            shape(terms, F32),
            shape(terms, F32),
            shape((2 * KMODE, atoms), BF),
            shape((16, atoms), F32),
        ),
        (),
        (held,),
        far_scratch(channels, atoms, spaces) + [table, long_rows],
        "half",
        COST["half"],
    )
    scaled, modes, longs = call(
        functools.partial(scaled_kernel, length),
        (
            shape((channels, atoms), BF),
            shape((2 * KMODE, spaces // 2 * atoms), BF),
            shape((16, spaces // 2 * atoms), F32),
        ),
        (),
        (held_rest, near_grad, weight, gain, cot_sums, modes_own, longs_own, scalar),
        far_scratch(channels, atoms, spaces),
        "scaled",
        COST["scaled"],
    )
    scaled_pieces = chan_pieces(scaled, scaled)
    messages, token = call(
        messages_kernel,
        (shape((NHARM, channels, atoms), BF), shape((8, 128), F32)),
        (),
        (
            held_rest,
            scalar,
            rest,
            coord,
            weight,
            source_sums,
            modes_own,
            longs_own,
            modes,
            longs,
        ),
        far_scratch(channels, atoms, spaces),
        "messages",
        COST["messages"],
    )
    grad_features = call(
        final_kernel if chans > 2 else two_chan(final_kernel, 4),
        shape((channels, atoms), F32),
        (lane,),
        (w_copy, *scaled_pieces, token),
        [pltpu.VMEM((chans * channels, atoms), BF)],
        "final",
        COST["final"],
    )
    return (messages, grad_features)


def mode_weights(wave_ref, length, total):
    k = wave_ref[...]
    count = k.shape[1]
    k = jnp.where(k[0:1] < 0, -k, k)
    k1, k2, k3 = k[0:1], k[1:2], k[2:3]
    code = jnp.where(k3 == 4, 76 + k2, (k2 + 4) * 8 + k3 + 4)
    rows = lax.broadcasted_iota(jnp.int32, (KMODE, count), 0)
    hot = (rows == code).astype(F32).astype(BF)
    longs = lax.broadcasted_iota(jnp.int32, (16, count), 0)
    hot1 = (longs == k1).astype(F32).astype(BF)
    mult = dot_nt(hot1, hot)
    lane = lax.broadcasted_iota(jnp.int32, (16, KMODE), 1)
    row = lax.broadcasted_iota(jnp.int32, (16, KMODE), 0)
    g2 = jnp.where(lane < 72, lane // 8 - 4, lane - 76).astype(F32)
    g3 = jnp.where(lane < 72, lane % 8 - 4, 4).astype(F32)
    f1 = row.astype(F32) * (2.0 * math.pi / length)
    f2 = g2 * (2.0 * math.pi / SIDE_WIDTH)
    f3 = g3 * (2.0 * math.pi / GAP_HEIGHT)
    ksq = f1 * f1 + f2 * f2 + f3 * f3
    value = jnp.exp(-0.5 * ksq) / (ksq + SCREEN * SCREEN) * (1.0 / math.sqrt(count * total))
    return jnp.where(mult > 0.0, mult * value, 0.0)


def phase_rows(x, y, z, length):
    atoms = x.shape[1]
    step = lax.broadcasted_iota(jnp.int32, (8, atoms), 0).astype(F32)
    first = sincos_turns((step + 1.0) * (x * (1.0 / length)))
    second = sincos_turns((step - 4.0) * (y * (1.0 / SIDE_WIDTH)))
    third = sincos_turns((step - 4.0) * (z * (1.0 / GAP_HEIGHT)))
    return first, second, third


def mode_table(second, third):
    c2, s2 = second
    c3, s3 = third
    atoms = c2.shape[1]
    cos, sin = [], []
    for k2 in range(9):
        a = c2[k2 : k2 + 1] if k2 < 8 else c2[0:1]
        b = s2[k2 : k2 + 1] if k2 < 8 else -s2[0:1]
        cos.append(a * c3 - b * s3)
        sin.append(a * s3 + b * c3)
    a, b = c3[0:1], -s3[0:1]
    cos.append(c2 * a - s2 * b)
    sin.append(c2 * b + s2 * a)
    one = lax.broadcasted_iota(jnp.int32, (8, atoms), 0) == 0
    cos.append(jnp.where(one, c2[0:1] * a + s2[0:1] * b, 0.0))
    sin.append(jnp.where(one, c2[0:1] * b - s2[0:1] * a, 0.0))
    pad = jnp.zeros((KMODE - 88, atoms), F32)
    return jnp.concatenate(cos + [pad] + sin + [pad], 0).astype(BF)


def unpack_pos(tail):
    t = tail.astype(F32)
    pos = (t[0:3] + t[3:6]) + t[6:9]
    return pos[0:1], pos[1:2], pos[2:3]


def solution(mesh):
    return jax.shard_map(
        on_device,
        mesh=mesh,
        in_specs=(
            P("chan", "space"),
            P(None, "space"),
            P("space"),
            P("space"),
            P("space"),
            P("space"),
            P("space"),
            P(),
            P(None, "chan"),
            P(),
            P(None, "chan"),
            P(None, "chan", "space"),
        ),
        out_specs=(P(None, "chan", "space"), P("chan", "space")),
        check_vma=False,
    )
```

```python
import functools
import math

import jax
import jax.numpy as jnp
from jax import lax
from jax.experimental import pallas as pl
from jax.experimental.pallas import tpu as pltpu
from jax.sharding import PartitionSpec as P

NSPEC = 6
BLOCK = 64
REACH = 4
NRAD = 16
NHARM = 9
KLONG = 8
KMODE = 128
MID = NRAD // 2

SLICE_WIDTH = 0.5
CUTOFF = SLICE_WIDTH * REACH
SIDE_WIDTH = 12.0
GAP_HEIGHT = 24.0
SIDE_CENTRE = 0.75
SCREEN = 0.5
HIGH = lax.Precision.HIGHEST
BF = jnp.bfloat16
F32 = jnp.float32
R3 = math.sqrt(3.0)
R5 = math.sqrt(5.0)
R15 = math.sqrt(15.0)

COST = dict(prep=1, source=1, radial=3, near_grad=3, near_messages=4, scaled=2, half=0.2, messages=2, final=1)
VMEM = pl.BlockSpec(memory_space=pltpu.VMEM)
SMEM = pl.BlockSpec(memory_space=pltpu.SMEM)


def dot_nt(a, b):
    return lax.dot_general(a, b, (((1,), (1,)), ((), ())), preferred_element_type=F32)


def dot_nn(a, b):
    return lax.dot_general(a, b, (((1,), (0,)), ((), ())), preferred_element_type=F32)


def harmonic_rows(x, y, z):
    s = x * x + y * y + z * z
    return [
        None,
        R3 * x,
        R3 * y,
        R3 * z,
        R15 * x * y,
        R15 * y * z,
        0.5 * R5 * (3.0 * z * z - s),
        R15 * x * z,
        0.5 * R15 * (x * x - y * y),
    ]


def shift_terms(x, y, z):
    q = R15 / R3
    return {
        (1, 0): -R3 * x,
        (2, 0): -R3 * y,
        (3, 0): -R3 * z,
        (4, 1): -q * y,
        (4, 2): -q * x,
        (4, 0): R15 * x * y,
        (5, 3): -q * y,
        (5, 2): -q * z,
        (5, 0): R15 * y * z,
        (6, 3): (-2.0 * R5 / R3) * z,
        (6, 1): (R5 / R3) * x,
        (6, 2): (R5 / R3) * y,
        (6, 0): 0.5 * R5 * (2.0 * z * z - x * x - y * y),
        (7, 3): -q * x,
        (7, 1): -q * z,
        (7, 0): R15 * x * z,
        (8, 1): -q * x,
        (8, 2): q * y,
        (8, 0): 0.5 * R15 * (x * x - y * y),
    }


def sincos_turns(turns):
    r = turns - jnp.floor(turns + 0.5)
    x = r * math.pi
    x2 = x * x
    s = jnp.full_like(x, -1.0 / math.factorial(11))
    for k, sign in ((9, 1.0), (7, -1.0), (5, 1.0), (3, -1.0), (1, 1.0)):
        s = s * x2 + sign / math.factorial(k)
    s = s * x
    c = jnp.full_like(x, 1.0 / math.factorial(12))
    for k, sign in ((10, -1.0), (8, 1.0), (6, -1.0), (4, 1.0), (2, -1.0), (0, 1.0)):
        c = c * x2 + sign / math.factorial(k)
    return 1.0 - 2.0 * s * s, 2.0 * s * c


def valid_row(count_ref, atoms):
    lane = lax.broadcasted_iota(jnp.int32, (1, atoms), 1)
    limit = jnp.zeros((1, atoms), jnp.int32)
    for b in range(atoms // BLOCK):
        limit = jnp.where(lane // BLOCK == b, count_ref[b] + b * BLOCK, limit)
    return (lane < limit).astype(F32)


def gain_rows(species_ref, species_gain_ref):
    ids = species_ref[...]
    rows = lax.broadcasted_iota(jnp.int32, (8, ids.shape[1]), 0)
    onehot = (rows == ids).astype(F32)[:NSPEC]
    return lax.dot_general(
        species_gain_ref[...],
        onehot,
        (((0,), (0,)), ((), ())),
        precision=HIGH,
        preferred_element_type=F32,
    )


def tail_rows(pos, flags, valid):
    atoms = pos.shape[1]
    top = pos.astype(BF).astype(F32)
    rest = pos - top
    mid = rest.astype(BF).astype(F32)
    low = rest - mid
    return jnp.concatenate([top, mid, low, flags, valid, jnp.zeros((5, atoms), F32)], 0).astype(BF)


def prep_kernel(
    live_ref,
    count_hbm,
    home_hbm,
    reach_hbm,
    pos_hbm,
    cot_hbm,
    species_hbm,
    gain_hbm,
    feats_hbm,
    w_hbm,
    head_ref,
    gain_ref,
    feats_ref,
    w_ref,
    count_ref,
    home_ref,
    reach_ref,
    pos_ref,
    species_ref,
    species_gain_ref,
    sems,
):
    channels, atoms = feats_hbm.shape
    pairs = (
        (count_hbm, count_ref),
        (home_hbm, home_ref),
        (reach_hbm, reach_ref),
        (pos_hbm, pos_ref),
        (species_hbm, species_ref),
        (gain_hbm, species_gain_ref),
        (cot_hbm.at[0:channels, :], head_ref.at[0:channels, :]),
        (feats_hbm, feats_ref),
        (w_hbm, w_ref),
    )
    copies = [pltpu.make_async_copy(a, b, sems.at[i]) for i, (a, b) in enumerate(pairs)]
    for copy in copies:
        copy.start()
    for copy in copies[:6]:
        copy.wait()
    lane = lax.broadcasted_iota(jnp.int32, (1, atoms), 1)
    flags = jnp.zeros((1, atoms), F32)
    for p in range(home_ref.shape[0]):
        slot = home_ref[p] * REACH + reach_ref[p] - 1
        flags = jnp.where(jnp.logical_and(lane == slot, p < live_ref[0]), 1.0, flags)
    valid = valid_row(count_ref, atoms)
    head_ref[channels:, :] = tail_rows(pos_ref[...], flags, valid)
    gain_ref[...] = gain_rows(species_ref, species_gain_ref) * valid
    for copy in copies[6:]:
        copy.wait()


def source_kernel(chans, lane_ref, *refs):
    pieces, (w_ref, gain_ref, head_ref) = refs[:chans], refs[chans : chans + 3]
    out_ref, all_ref, mix_ref = refs[-3:]
    channels = gain_ref.shape[0]
    lane = lane_ref[0]
    out_ref[0 : channels + 16, :] = head_ref[...]
    for m, piece in enumerate(pieces):
        at = pl.multiple_of((lane ^ m) * channels, channels)
        all_ref[pl.ds(at, channels), :] = piece[...]
    mix_ref[...] = lax.dot_general(
        w_ref[...], all_ref[...], (((0,), (0,)), ((), ())), preferred_element_type=F32
    )
    mixed = mix_ref[pl.ds(pl.multiple_of(lane * channels, channels), channels), :]
    out_ref[channels + 16 :, :] = (mixed * gain_ref[...]).astype(BF)


def geometry(place, spaces, halos, tiles, channels, cols_ref, live_ref, coord_ref):
    atoms = halos[0].shape[1]
    blocks = atoms // BLOCK
    length = SLICE_WIDTH * blocks * spaces
    even = lax.rem(place, 2) == 0
    wrap = jnp.where(place == 0, -length, jnp.where(place == spaces - 1, length, 0.0))
    centre = (place.astype(F32) + 0.5) * (SLICE_WIDTH * blocks)
    lane = lax.broadcasted_iota(jnp.int32, (1, atoms), 1)
    home = lane // BLOCK
    none = jnp.zeros((1, atoms), F32)

    def tail_of(halo):
        cut = halo.shape[0] - channels
        return halo[cut - 16 : cut, :]

    def flag_row(tail, h, r):
        index = h * REACH + r - 1
        return jnp.broadcast_to(tail[9:10, index : index + 1].astype(F32), (1, atoms))

    def coords_of(t, tail):
        x, y, z = unpack_pos(tail)
        x = x - (centre - wrap) if t == 2 else x - centre
        x = x * (1.0 / CUTOFF)
        y = (y - SIDE_CENTRE) * (1.0 / CUTOFF)
        z = (z - SIDE_CENTRE) * (1.0 / CUTOFF)
        return x, y, z

    own_tail = tail_of(halos[0])
    own = coords_of(0, own_tail)
    for i, t in enumerate(tiles):
        tail = tail_of(halos[t])
        valid = tail[10:11].astype(F32)
        padded = jnp.concatenate([*coords_of(t, tail), valid, jnp.zeros((4, atoms), F32)], 0)
        coord_ref[i] = padded
        cols_ref[i * atoms : (i + 1) * atoms, :] = padded.T
        for e in range(blocks):
            row = none
            if t == 0:
                for h in range(blocks):
                    d = abs(e - h)
                    value = none + 1.0 if d == 0 else flag_row(tail, min(e, h), d)
                    row = jnp.where(home == h, value, row)
            else:
                behind = none
                for h in range(blocks):
                    if e + blocks - h <= REACH:
                        row = jnp.where(home == h, flag_row(own_tail, h, e + blocks - h), row)
                    if h + blocks - e <= REACH:
                        behind = jnp.where(home == h, flag_row(tail, e, h + blocks - e), behind)
                row = jnp.where(even if t == 1 else jnp.logical_not(even), row, behind)
            live_ref[i * blocks + e : i * blocks + e + 1, :] = row
    return own


def fill_radial(own, tiles, cols_ref, live_ref, radial_ref):
    xa, ya, za = own
    atoms = xa.shape[1]
    chunk = BLOCK
    for index in range(len(tiles) * atoms // chunk):
        lo = index * chunk
        at = slice(lo, lo + chunk)
        col = cols_ref[at, :]
        dx = col[:, 0:1] - xa
        dy = col[:, 1:2] - ya
        dz = col[:, 2:3] - za
        s = jnp.minimum(dx * dx + dy * dy + dz * dz, 1.0)
        gap = 1.0 - s
        envelope = gap * gap * live_ref[index : index + 1, :]
        if tiles[lo // atoms] == 0:
            other = lax.broadcasted_iota(jnp.int32, (chunk, atoms), 0) + lo
            me = lax.broadcasted_iota(jnp.int32, (chunk, atoms), 1)
            envelope = jnp.where(other == me, 0.0, envelope)
        off = s - MID / (NRAD - 1)
        middle = envelope * jnp.exp(-0.5 * (NRAD - 1) ** 2 * (off * off))
        radial_ref[MID, at, :] = middle.astype(BF)
        grow = jnp.exp((NRAD - 1.0) * s)
        value = middle
        for n in range(MID, NRAD - 1):
            value = value * (grow * math.exp(-(2 * n + 1) / 2))
            radial_ref[n + 1, at, :] = value.astype(BF)
        shrink = jnp.exp((1.0 - NRAD) * s)
        value = middle
        for n in range(MID, 0, -1):
            value = value * (shrink * math.exp((2 * n - 1) / 2))
            radial_ref[n - 1, at, :] = value.astype(BF)


def radial_kernel(
    spaces,
    place_ref,
    own_ref,
    first_ref,
    wave_ref,
    w_rad_ref,
    radial_ref,
    coord_ref,
    filt_ref,
    weight_ref,
    cols_ref,
    live_ref,
):
    atoms = own_ref.shape[1]
    length = SLICE_WIDTH * (atoms // BLOCK) * spaces
    channels = w_rad_ref.shape[1]
    halos = (own_ref, first_ref)
    own = geometry(
        place_ref[0], spaces, halos, (0, 1), channels, cols_ref, live_ref, coord_ref
    )
    w_cols = w_rad_ref[...].T
    for n in range(NRAD):
        filt_ref[n] = jnp.broadcast_to(w_cols[:, n : n + 1], filt_ref.shape[1:])
    fill_radial(own, (0, 1), cols_ref, live_ref, radial_ref)
    weight_ref[...] = mode_weights(wave_ref, length, atoms * spaces)


def radial_other_kernel(
    spaces, place_ref, own_ref, second_ref, filt_ref, radial_ref, coord_ref, cols_ref, live_ref
):
    halos = (own_ref, None, second_ref)
    channels = filt_ref.shape[1]
    own = geometry(place_ref[0], spaces, halos, (2,), channels, cols_ref, live_ref, coord_ref)
    fill_radial(own, (2,), cols_ref, live_ref, radial_ref)


def near_mix(left_ref, radial_ref, radial_other_ref, filt_ref, total_ref):
    cut = radial_ref.shape[1]
    for n in range(NRAD):
        part = dot_nn(left_ref[:, 0:cut], radial_ref[n])
        part = part + dot_nn(left_ref[:, cut:], radial_other_ref[n])
        part = part.reshape(total_ref.shape) * filt_ref[n][None]
        if n == 0:
            total_ref[...] = part
        else:
            total_ref[...] += part


def near_scratch(channels, atoms):
    return [
        pltpu.VMEM((NHARM * channels, 3 * atoms), BF),
        pltpu.VMEM((NHARM, channels, atoms), F32),
    ]


def coord_tile(coord_ref, coord_other_ref, t):
    return coord_ref[t] if t < 2 else coord_other_ref[0]


def coord_rows(coord_ref, coord_other_ref, t):
    tile = coord_tile(coord_ref, coord_other_ref, t)
    return (tile[0:1], tile[1:2], tile[2:3])


def near_grad_kernel(
    own_ref,
    first_ref,
    second_ref,
    radial_ref,
    radial_other_ref,
    coord_ref,
    coord_other_ref,
    filt_ref,
    grad_ref,
    left_ref,
    total_ref,
):
    channels, atoms = grad_ref.shape
    for t, halo in enumerate((own_ref, first_ref, second_ref)):
        at = slice(t * atoms, (t + 1) * atoms)
        valid = coord_tile(coord_ref, coord_other_ref, t)[3:4]
        grads = [
            halo[l * channels : (l + 1) * channels, :].astype(F32) * valid for l in range(NHARM)
        ]
        moved = list(grads)
        for (l, m), term in shift_terms(*coord_rows(coord_ref, coord_other_ref, t)).items():
            moved[m] = moved[m] + grads[l] * term
        for m in range(NHARM):
            left_ref[m * channels : (m + 1) * channels, at] = moved[m].astype(BF)
    near_mix(left_ref, radial_ref, radial_other_ref, filt_ref, total_ref)
    harm = harmonic_rows(*coord_rows(coord_ref, coord_other_ref, 0))
    grad = total_ref[0]
    for m in range(1, NHARM):
        grad = grad + total_ref[m] * harm[m]
    grad_ref[...] = grad


def fill_terms(data, cos, sin, terms_ref, at):
    channels = data.shape[0]
    terms_ref[0:channels, at] = data.astype(BF)
    for k in range(KLONG):
        lo = (1 + 2 * k) * channels
        terms_ref[lo : lo + channels, at] = (data * cos[k : k + 1]).astype(BF)
        terms_ref[lo + channels : lo + 2 * channels, at] = (data * sin[k : k + 1]).astype(BF)


def gathered_sums(fill, pairs, terms_ref, modes_ref):
    span = terms_ref.shape[1]
    group = pairs * span // modes_ref.shape[1]
    sums = None
    for base in range(0, pairs, group):
        lax.fori_loop(0, group, fill, base)
        at = slice(base // group * span, (base // group + 1) * span)
        part = dot_nt(terms_ref[...], modes_ref[:, at])
        sums = part if sums is None else sums + part
    return sums


def far_field(sums, weight_ref, own_ref, own_longs_ref, channels):
    rows_re, rows_im = [], []
    for k in range(KLONG + 1):
        w = weight_ref[k : k + 1, :]
        if k == 0:
            real = sums[0:channels]
            cos, sin = real[:, :KMODE], real[:, KMODE:]
        else:
            lo = (2 * k - 1) * channels
            real, imag = sums[lo : lo + channels], sums[lo + channels : lo + 2 * channels]
            cos = real[:, :KMODE] - imag[:, KMODE:]
            sin = real[:, KMODE:] + imag[:, :KMODE]
        cos, sin = cos * w, sin * w
        rows_re.append(jnp.concatenate([cos, sin], 1))
        if k > 0:
            rows_im.append(jnp.concatenate([sin, -cos], 1))
    waves = jnp.concatenate(rows_re + rows_im, 0).astype(BF)
    back = dot_nn(waves, own_ref[...])
    cos, sin = own_longs_ref[0:8, :], own_longs_ref[8:16, :]
    far = back[0:channels]
    for k in range(KLONG):
        lo = (1 + k) * channels
        far = far + back[lo : lo + channels] * cos[k : k + 1]
        lo = (1 + KLONG + k) * channels
        far = far + back[lo : lo + channels] * sin[k : k + 1]
    return far


def far_scratch(channels, atoms, spaces):
    return [pltpu.VMEM(((2 * KLONG + 1) * channels, min(spaces // 2, 8) * atoms), BF)]


def cot_filler(length, held_ref, channels, modes_ref, longs_ref, terms_ref):
    unit = 2 * channels + 16
    atoms = held_ref.shape[2]

    def fill(p, base):
        for q in range(2):
            lo = q * unit
            tail = held_ref[base + p, lo + channels : lo + channels + 16, :]
            first, second, third = phase_rows(*unpack_pos(tail), length)
            at = pl.ds(pl.multiple_of((2 * (base + p) + q) * atoms, atoms), atoms)
            modes_ref[:, at] = mode_table(second, third)
            longs_ref[0:8, at] = first[0]
            longs_ref[8:16, at] = first[1]
            cot = held_ref[base + p, lo : lo + channels, :].astype(F32)
            at = pl.ds(pl.multiple_of((2 * p + q) * atoms, atoms), atoms)
            fill_terms(cot * tail[10:11].astype(F32), *first, terms_ref, at)
        return base

    return fill


def source_filler(held_ref, channels, longs_ref, terms_ref):
    unit = 2 * channels + 16
    atoms = held_ref.shape[2]

    def fill(p, base):
        for q in range(2):
            lo = q * unit + channels + 16
            data = held_ref[base + p, lo : lo + channels, :].astype(F32)
            at = pl.ds(pl.multiple_of((2 * (base + p) + q) * atoms, atoms), atoms)
            cos, sin = longs_ref[0:8, at], longs_ref[8:16, at]
            at = pl.ds(pl.multiple_of((2 * p + q) * atoms, atoms), atoms)
            fill_terms(data, cos, sin, terms_ref, at)
        return base

    return fill


def half_kernel(
    length,
    held_ref,
    cot_sums_ref,
    source_sums_ref,
    own_ref,
    own_longs_ref,
    terms_ref,
    modes_ref,
    longs_ref,
):
    pairs, rows, atoms = held_ref.shape
    channels = (rows // 2 - 16) // 2
    fill = cot_filler(length, held_ref, channels, modes_ref, longs_ref, terms_ref)
    cot_sums_ref[...] = gathered_sums(fill, pairs, terms_ref, modes_ref)
    fill = source_filler(held_ref, channels, longs_ref, terms_ref)
    source_sums_ref[...] = gathered_sums(fill, pairs, terms_ref, modes_ref)
    own_ref[...] = modes_ref[:, 0:atoms]
    own_longs_ref[...] = longs_ref[:, 0:atoms]


def scaled_kernel(
    length,
    rest_ref,
    near_ref,
    weight_ref,
    gain_ref,
    sums_ref,
    own_ref,
    own_longs_ref,
    order_ref,
    scaled_ref,
    modes_ref,
    longs_ref,
    terms_ref,
):
    channels = near_ref.shape[0]
    fill = cot_filler(length, rest_ref, channels, modes_ref, longs_ref, terms_ref)
    sums = gathered_sums(fill, rest_ref.shape[0], terms_ref, modes_ref) + sums_ref[...]
    far = far_field(sums, weight_ref, own_ref, own_longs_ref, channels)
    scaled_ref[...] = ((near_ref[...] + far) * gain_ref[...]).astype(BF)


def near_messages_kernel(
    own_ref,
    first_ref,
    second_ref,
    radial_ref,
    radial_other_ref,
    coord_ref,
    coord_other_ref,
    filt_ref,
    scalar_ref,
    rest_ref,
    left_ref,
    total_ref,
):
    channels, atoms = scalar_ref.shape
    for t, ref in enumerate((own_ref, first_ref, second_ref)):
        lo = ref.shape[0] - channels
        at = slice(t * atoms, (t + 1) * atoms)
        left_ref[0:channels, at] = ref[lo : lo + channels, :]
        source = ref[lo : lo + channels, :].astype(F32)
        harm = harmonic_rows(*coord_rows(coord_ref, coord_other_ref, t))
        for m in range(1, NHARM):
            left_ref[m * channels : (m + 1) * channels, at] = (source * harm[m]).astype(BF)
    near_mix(left_ref, radial_ref, radial_other_ref, filt_ref, total_ref)
    valid = coord_ref[0][3:4]
    sums = [total_ref[m] for m in range(NHARM)]
    near = list(sums)
    for (l, m), term in shift_terms(*coord_rows(coord_ref, coord_other_ref, 0)).items():
        near[l] = near[l] + sums[m] * term
    scalar_ref[...] = near[0] * valid
    for l in range(1, NHARM):
        rest_ref[l - 1] = (near[l] * valid).astype(BF)


def messages_kernel(
    held_ref,
    scalar_ref,
    rest_ref,
    coord_ref,
    weight_ref,
    sums_ref,
    own_ref,
    own_longs_ref,
    modes_ref,
    longs_ref,
    messages_ref,
    token_ref,
    terms_ref,
):
    channels = scalar_ref.shape[0]
    fill = source_filler(held_ref, channels, longs_ref, terms_ref)
    sums = gathered_sums(fill, held_ref.shape[0], terms_ref, modes_ref) + sums_ref[...]
    far = far_field(sums, weight_ref, own_ref, own_longs_ref, channels)
    valid = coord_ref[0][3:4]
    messages_ref[0] = (scalar_ref[...] + far * valid).astype(BF)
    messages_ref[1:NHARM] = rest_ref[...]
    token_ref[...] = jnp.zeros_like(token_ref)


def final_kernel(
    lane_ref, w_ref, own_ref, first_ref, other_ref, token_ref, out_ref, all_ref
):
    channels = out_ref.shape[0]
    lane = lane_ref[0]
    pieces = [own_ref[...], first_ref[...]]
    if other_ref is not None:
        pieces += [other_ref[m * channels : (m + 1) * channels, :] for m in range(2)]
    for m, piece in enumerate(pieces):
        at = pl.multiple_of((lane ^ m) * channels, channels)
        all_ref[pl.ds(at, channels), :] = piece
    first = pl.multiple_of(lane * channels, channels)
    out_ref[...] = dot_nn(w_ref[pl.ds(first, channels), :], all_ref[...])


def two_chan(kernel, place):
    def without(*refs):
        kernel(*refs[:place], None, *refs[place:])

    return without


def cost(micros):
    return pl.CostEstimate(
        flops=int(micros * 1e9), bytes_accessed=int(micros * 3e6), transcendentals=0
    )


def swapped(block, axis, bit):
    return lax.ppermute(block, axis, [(i, i ^ bit) for i in range(lax.axis_size(axis))])


def chan_pieces(raw, kept):
    first = swapped(raw, "chan", 1)
    if lax.axis_size("chan") == 2:
        return [kept, first]
    return [kept, first, swapped(jnp.concatenate([kept, first], 0), "chan", 2)]


def on_device(
    features,
    positions,
    species,
    block_count,
    pair_home,
    pair_reach,
    pair_count,
    wave_ints,
    species_gain,
    w_in,
    w_rad,
    cotangent,
):
    channels, atoms = features.shape
    spaces = lax.axis_size("space")
    chans = lax.axis_size("chan")
    length = SLICE_WIDTH * (atoms // BLOCK) * spaces
    place = lax.axis_index("space").astype(jnp.int32).reshape(1)
    lane = lax.axis_index("chan").astype(jnp.int32).reshape(1)
    species = species.reshape(1, atoms)
    shape = jax.ShapeDtypeStruct

    def call(kernel, out_shape, smem, vmem, scratch, name, micros):
        return pl.pallas_call(
            kernel,
            out_shape=out_shape,
            in_specs=[SMEM] * len(smem) + [VMEM] * len(vmem),
            out_specs=jax.tree.map(lambda _: VMEM, out_shape),
            scratch_shapes=scratch,
            compiler_params=pltpu.CompilerParams(vmem_limit_bytes=32 * 1024 * 1024),
            cost_estimate=cost(micros),
            name=name,
        )(*smem, *vmem)

    def in_hbm(x):
        return pltpu.with_memory_space_constraint(x, pltpu.HBM)

    cots = cotangent.reshape(NHARM * channels, atoms)
    head, gain, feats_copy, w_copy = pl.pallas_call(
        prep_kernel,
        out_shape=(
            shape((channels + 16, atoms), BF),
            shape((channels, atoms), F32),
            shape(features.shape, BF),
            shape(w_in.shape, BF),
        ),
        in_specs=[SMEM] + [pl.BlockSpec(memory_space=pltpu.HBM)] * 9,
        out_specs=(VMEM,) * 4,
        scratch_shapes=[
            pltpu.SMEM(block_count.shape, jnp.int32),
            pltpu.SMEM(pair_home.shape, jnp.int32),
            pltpu.SMEM(pair_reach.shape, jnp.int32),
            pltpu.VMEM(positions.shape, F32),
            pltpu.VMEM(species.shape, jnp.int32),
            pltpu.VMEM(species_gain.shape, F32),
            pltpu.SemaphoreType.DMA((9,)),
        ],
        compiler_params=pltpu.CompilerParams(vmem_limit_bytes=8 * 1024 * 1024),
        cost_estimate=cost(COST["prep"]),
        name="prep",
    )(
        pair_count,
        *[
            in_hbm(x)
            for x in (
                block_count,
                pair_home,
                pair_reach,
                positions,
                cots,
                species,
                species_gain,
                features,
                w_in,
            )
        ]
    )
    pieces = [feats_copy] + [swapped(features, "chan", m) for m in range(1, chans)]
    other = [i - 1 if i % 2 == 0 else i + 1 for i in range(spaces)]
    route = [(i, other[i] % spaces) for i in range(spaces)]
    second = lax.ppermute(cots, "space", route)
    first = swapped(cots, "space", 1)
    unit = call(
        functools.partial(source_kernel, chans),
        shape((2 * channels + 16, atoms), BF),
        (lane,),
        (*pieces, w_copy, gain, head, first, second),
        [pltpu.VMEM((w_in.shape[0], atoms), BF), pltpu.VMEM((w_in.shape[1], atoms), F32)],
        "source",
        COST["source"],
    )
    unit_first = swapped(unit, "space", 1)
    unit_second = lax.ppermute(unit[channels:], "space", route)
    block = jnp.concatenate([unit, unit_first], 0)
    held = block[None]
    bit = spaces // 2
    while bit > 2:
        held = jnp.concatenate([held, swapped(held, "space", bit)], 0)
        bit //= 2
    held_rest = swapped(held, "space", 2)
    radial, coord, filt, weight = call(
        functools.partial(radial_kernel, spaces),
        (
            shape((NRAD, 2 * atoms, atoms), BF),
            shape((2, 8, atoms), F32),
            shape((NRAD, channels, atoms), F32),
            shape((16, KMODE), F32),
        ),
        (place,),
        (unit, unit_first, wave_ints, w_rad),
        [pltpu.VMEM((2 * atoms, 8), F32), pltpu.VMEM((16, atoms), F32)],
        "radial",
        COST["radial"],
    )
    radial_other, coord_other = call(
        functools.partial(radial_other_kernel, spaces),
        (shape((NRAD, atoms, atoms), BF), shape((1, 8, atoms), F32)),
        (place,),
        (unit, unit_second, filt),
        [pltpu.VMEM((atoms, 8), F32), pltpu.VMEM((16, atoms), F32)],
        "radial_other",
        1,
    )
    near_grad = call(
        near_grad_kernel,
        shape((channels, atoms), F32),
        (),
        (cots, first, second, radial, radial_other, coord, coord_other, filt),
        near_scratch(channels, atoms),
        "near_grad",
        COST["near_grad"],
    )
    scalar, rest = call(
        near_messages_kernel,
        (shape((channels, atoms), F32), shape((NHARM - 1, channels, atoms), BF)),
        (),
        (unit, unit_first, unit_second, radial, radial_other, coord, coord_other, filt),
        near_scratch(channels, atoms),
        "near_messages",
        COST["near_messages"],
    )
    terms = ((2 * KLONG + 1) * channels, 2 * KMODE)
    table = pltpu.VMEM((2 * KMODE, spaces // 2 * atoms), BF)
    long_rows = pltpu.VMEM((16, spaces // 2 * atoms), F32)
    cot_sums, source_sums, modes_own, longs_own = call(
        functools.partial(half_kernel, length),
        (
            shape(terms, F32),
            shape(terms, F32),
            shape((2 * KMODE, atoms), BF),
            shape((16, atoms), F32),
        ),
        (),
        (held,),
        far_scratch(channels, atoms, spaces) + [table, long_rows],
        "half",
        COST["half"],
    )
    scaled, modes, longs = call(
        functools.partial(scaled_kernel, length),
        (
            shape((channels, atoms), BF),
            shape((2 * KMODE, spaces // 2 * atoms), BF),
            shape((16, spaces // 2 * atoms), F32),
        ),
        (),
        (held_rest, near_grad, weight, gain, cot_sums, modes_own, longs_own, scalar),
        far_scratch(channels, atoms, spaces),
        "scaled",
        COST["scaled"],
    )
    scaled_pieces = chan_pieces(scaled, scaled)
    messages, token = call(
        messages_kernel,
        (shape((NHARM, channels, atoms), BF), shape((8, 128), F32)),
        (),
        (
            held_rest,
            scalar,
            rest,
            coord,
            weight,
            source_sums,
            modes_own,
            longs_own,
            modes,
            longs,
        ),
        far_scratch(channels, atoms, spaces),
        "messages",
        COST["messages"],
    )
    grad_features = call(
        final_kernel if chans > 2 else two_chan(final_kernel, 4),
        shape((channels, atoms), F32),
        (lane,),
        (w_copy, *scaled_pieces, token),
        [pltpu.VMEM((chans * channels, atoms), BF)],
        "final",
        COST["final"],
    )
    return (messages, grad_features)


def mode_weights(wave_ref, length, total):
    k = wave_ref[...]
    count = k.shape[1]
    k = jnp.where(k[0:1] < 0, -k, k)
    k1, k2, k3 = k[0:1], k[1:2], k[2:3]
    code = jnp.where(k3 == 4, 76 + k2, (k2 + 4) * 8 + k3 + 4)
    rows = lax.broadcasted_iota(jnp.int32, (KMODE, count), 0)
    hot = (rows == code).astype(F32).astype(BF)
    longs = lax.broadcasted_iota(jnp.int32, (16, count), 0)
    hot1 = (longs == k1).astype(F32).astype(BF)
    mult = dot_nt(hot1, hot)
    lane = lax.broadcasted_iota(jnp.int32, (16, KMODE), 1)
    row = lax.broadcasted_iota(jnp.int32, (16, KMODE), 0)
    g2 = jnp.where(lane < 72, lane // 8 - 4, lane - 76).astype(F32)
    g3 = jnp.where(lane < 72, lane % 8 - 4, 4).astype(F32)
    f1 = row.astype(F32) * (2.0 * math.pi / length)
    f2 = g2 * (2.0 * math.pi / SIDE_WIDTH)
    f3 = g3 * (2.0 * math.pi / GAP_HEIGHT)
    ksq = f1 * f1 + f2 * f2 + f3 * f3
    value = jnp.exp(-0.5 * ksq) / (ksq + SCREEN * SCREEN) * (1.0 / math.sqrt(count * total))
    return jnp.where(mult > 0.0, mult * value, 0.0)


def phase_rows(x, y, z, length):
    atoms = x.shape[1]
    step = lax.broadcasted_iota(jnp.int32, (8, atoms), 0).astype(F32)
    first = sincos_turns((step + 1.0) * (x * (1.0 / length)))
    second = sincos_turns((step - 4.0) * (y * (1.0 / SIDE_WIDTH)))
    third = sincos_turns((step - 4.0) * (z * (1.0 / GAP_HEIGHT)))
    return first, second, third


def mode_table(second, third):
    c2, s2 = second
    c3, s3 = third
    atoms = c2.shape[1]
    cos, sin = [], []
    for k2 in range(9):
        a = c2[k2 : k2 + 1] if k2 < 8 else c2[0:1]
        b = s2[k2 : k2 + 1] if k2 < 8 else -s2[0:1]
        cos.append(a * c3 - b * s3)
        sin.append(a * s3 + b * c3)
    a, b = c3[0:1], -s3[0:1]
    cos.append(c2 * a - s2 * b)
    sin.append(c2 * b + s2 * a)
    one = lax.broadcasted_iota(jnp.int32, (8, atoms), 0) == 0
    cos.append(jnp.where(one, c2[0:1] * a + s2[0:1] * b, 0.0))
    sin.append(jnp.where(one, c2[0:1] * b - s2[0:1] * a, 0.0))
    pad = jnp.zeros((KMODE - 88, atoms), F32)
    return jnp.concatenate(cos + [pad] + sin + [pad], 0).astype(BF)


def unpack_pos(tail):
    t = tail.astype(F32)
    pos = (t[0:3] + t[3:6]) + t[6:9]
    return pos[0:1], pos[1:2], pos[2:3]


def solution(mesh):
    return jax.shard_map(
        on_device,
        mesh=mesh,
        in_specs=(
            P("chan", "space"),
            P(None, "space"),
            P("space"),
            P("space"),
            P("space"),
            P("space"),
            P("space"),
            P(),
            P(None, "chan"),
            P(),
            P(None, "chan"),
            P(None, "chan", "space"),
        ),
        out_specs=(P(None, "chan", "space"), P("chan", "space")),
        check_vma=False,
    )
```

```python
import functools
import math

import jax
import jax.numpy as jnp
from jax import lax
from jax.experimental import pallas as pl
from jax.experimental.pallas import tpu as pltpu
from jax.sharding import PartitionSpec as P

NSPEC = 6
BLOCK = 64
REACH = 4
NRAD = 16
NHARM = 9
KLONG = 8
KMODE = 128
MID = NRAD // 2

SLICE_WIDTH = 0.5
CUTOFF = SLICE_WIDTH * REACH
SIDE_WIDTH = 12.0
GAP_HEIGHT = 24.0
SIDE_CENTRE = 0.75
SCREEN = 0.5
HIGH = lax.Precision.HIGHEST
BF = jnp.bfloat16
F32 = jnp.float32
R3 = math.sqrt(3.0)
R5 = math.sqrt(5.0)
R15 = math.sqrt(15.0)

COST = dict(prep=1, source=1, radial=3, near_grad=3, near_messages=4, scaled=2, half=0.2, messages=2, final=1)
VMEM = pl.BlockSpec(memory_space=pltpu.VMEM)
SMEM = pl.BlockSpec(memory_space=pltpu.SMEM)


def dot_nt(a, b):
    return lax.dot_general(a, b, (((1,), (1,)), ((), ())), preferred_element_type=F32)


def dot_nn(a, b):
    return lax.dot_general(a, b, (((1,), (0,)), ((), ())), preferred_element_type=F32)


def harmonic_rows(x, y, z):
    s = x * x + y * y + z * z
    return [
        None,
        R3 * x,
        R3 * y,
        R3 * z,
        R15 * x * y,
        R15 * y * z,
        0.5 * R5 * (3.0 * z * z - s),
        R15 * x * z,
        0.5 * R15 * (x * x - y * y),
    ]


def shift_terms(x, y, z):
    q = R15 / R3
    return {
        (1, 0): -R3 * x,
        (2, 0): -R3 * y,
        (3, 0): -R3 * z,
        (4, 1): -q * y,
        (4, 2): -q * x,
        (4, 0): R15 * x * y,
        (5, 3): -q * y,
        (5, 2): -q * z,
        (5, 0): R15 * y * z,
        (6, 3): (-2.0 * R5 / R3) * z,
        (6, 1): (R5 / R3) * x,
        (6, 2): (R5 / R3) * y,
        (6, 0): 0.5 * R5 * (2.0 * z * z - x * x - y * y),
        (7, 3): -q * x,
        (7, 1): -q * z,
        (7, 0): R15 * x * z,
        (8, 1): -q * x,
        (8, 2): q * y,
        (8, 0): 0.5 * R15 * (x * x - y * y),
    }


def sincos_turns(turns):
    r = turns - jnp.floor(turns + 0.5)
    x = r * math.pi
    x2 = x * x
    s = jnp.full_like(x, -1.0 / math.factorial(11))
    for k, sign in ((9, 1.0), (7, -1.0), (5, 1.0), (3, -1.0), (1, 1.0)):
        s = s * x2 + sign / math.factorial(k)
    s = s * x
    c = jnp.full_like(x, 1.0 / math.factorial(12))
    for k, sign in ((10, -1.0), (8, 1.0), (6, -1.0), (4, 1.0), (2, -1.0), (0, 1.0)):
        c = c * x2 + sign / math.factorial(k)
    return 1.0 - 2.0 * s * s, 2.0 * s * c


def valid_row(count_ref, atoms):
    lane = lax.broadcasted_iota(jnp.int32, (1, atoms), 1)
    limit = jnp.zeros((1, atoms), jnp.int32)
    for b in range(atoms // BLOCK):
        limit = jnp.where(lane // BLOCK == b, count_ref[b] + b * BLOCK, limit)
    return (lane < limit).astype(F32)


def gain_rows(species_ref, species_gain_ref):
    ids = species_ref[...]
    rows = lax.broadcasted_iota(jnp.int32, (8, ids.shape[1]), 0)
    onehot = (rows == ids).astype(F32)[:NSPEC]
    return lax.dot_general(
        species_gain_ref[...],
        onehot,
        (((0,), (0,)), ((), ())),
        precision=HIGH,
        preferred_element_type=F32,
    )


def tail_rows(pos, flags, valid):
    atoms = pos.shape[1]
    top = pos.astype(BF).astype(F32)
    rest = pos - top
    mid = rest.astype(BF).astype(F32)
    low = rest - mid
    return jnp.concatenate([top, mid, low, flags, valid, jnp.zeros((5, atoms), F32)], 0).astype(BF)


def prep_kernel(
    live_ref,
    count_hbm,
    home_hbm,
    reach_hbm,
    pos_hbm,
    cot_hbm,
    species_hbm,
    gain_hbm,
    feats_hbm,
    w_hbm,
    head_ref,
    gain_ref,
    feats_ref,
    w_ref,
    count_ref,
    home_ref,
    reach_ref,
    pos_ref,
    species_ref,
    species_gain_ref,
    sems,
):
    channels, atoms = feats_hbm.shape
    pairs = (
        (count_hbm, count_ref),
        (home_hbm, home_ref),
        (reach_hbm, reach_ref),
        (pos_hbm, pos_ref),
        (species_hbm, species_ref),
        (gain_hbm, species_gain_ref),
        (cot_hbm.at[0:channels, :], head_ref.at[0:channels, :]),
        (feats_hbm, feats_ref),
        (w_hbm, w_ref),
    )
    copies = [pltpu.make_async_copy(a, b, sems.at[i]) for i, (a, b) in enumerate(pairs)]
    for copy in copies:
        copy.start()
    for copy in copies[:6]:
        copy.wait()
    lane = lax.broadcasted_iota(jnp.int32, (1, atoms), 1)
    flags = jnp.zeros((1, atoms), F32)
    for p in range(home_ref.shape[0]):
        slot = home_ref[p] * REACH + reach_ref[p] - 1
        flags = jnp.where(jnp.logical_and(lane == slot, p < live_ref[0]), 1.0, flags)
    valid = valid_row(count_ref, atoms)
    head_ref[channels:, :] = tail_rows(pos_ref[...], flags, valid)
    gain_ref[...] = gain_rows(species_ref, species_gain_ref) * valid
    for copy in copies[6:]:
        copy.wait()


def source_kernel(chans, lane_ref, *refs):
    pieces, (w_ref, gain_ref, head_ref) = refs[:chans], refs[chans : chans + 3]
    out_ref, all_ref, mix_ref = refs[-3:]
    channels = gain_ref.shape[0]
    lane = lane_ref[0]
    out_ref[0 : channels + 16, :] = head_ref[...]
    for m, piece in enumerate(pieces):
        at = pl.multiple_of((lane ^ m) * channels, channels)
        all_ref[pl.ds(at, channels), :] = piece[...]
    mix_ref[...] = lax.dot_general(
        w_ref[...], all_ref[...], (((0,), (0,)), ((), ())), preferred_element_type=F32
    )
    mixed = mix_ref[pl.ds(pl.multiple_of(lane * channels, channels), channels), :]
    out_ref[channels + 16 :, :] = (mixed * gain_ref[...]).astype(BF)


def geometry(place, spaces, halos, tiles, channels, cols_ref, live_ref, coord_ref):
    atoms = halos[0].shape[1]
    blocks = atoms // BLOCK
    length = SLICE_WIDTH * blocks * spaces
    even = lax.rem(place, 2) == 0
    wrap = jnp.where(place == 0, -length, jnp.where(place == spaces - 1, length, 0.0))
    centre = (place.astype(F32) + 0.5) * (SLICE_WIDTH * blocks)
    lane = lax.broadcasted_iota(jnp.int32, (1, atoms), 1)
    home = lane // BLOCK
    none = jnp.zeros((1, atoms), F32)

    def tail_of(halo):
        cut = halo.shape[0] - channels
        return halo[cut - 16 : cut, :]

    def flag_row(tail, h, r):
        index = h * REACH + r - 1
        return jnp.broadcast_to(tail[9:10, index : index + 1].astype(F32), (1, atoms))

    def coords_of(t, tail):
        x, y, z = unpack_pos(tail)
        x = x - (centre - wrap) if t == 2 else x - centre
        x = x * (1.0 / CUTOFF)
        y = (y - SIDE_CENTRE) * (1.0 / CUTOFF)
        z = (z - SIDE_CENTRE) * (1.0 / CUTOFF)
        return x, y, z

    own_tail = tail_of(halos[0])
    own = coords_of(0, own_tail)
    for i, t in enumerate(tiles):
        tail = tail_of(halos[t])
        valid = tail[10:11].astype(F32)
        padded = jnp.concatenate([*coords_of(t, tail), valid, jnp.zeros((4, atoms), F32)], 0)
        coord_ref[i] = padded
        cols_ref[i * atoms : (i + 1) * atoms, :] = padded.T
        for e in range(blocks):
            row = none
            if t == 0:
                for h in range(blocks):
                    d = abs(e - h)
                    value = none + 1.0 if d == 0 else flag_row(tail, min(e, h), d)
                    row = jnp.where(home == h, value, row)
            else:
                behind = none
                for h in range(blocks):
                    if e + blocks - h <= REACH:
                        row = jnp.where(home == h, flag_row(own_tail, h, e + blocks - h), row)
                    if h + blocks - e <= REACH:
                        behind = jnp.where(home == h, flag_row(tail, e, h + blocks - e), behind)
                row = jnp.where(even if t == 1 else jnp.logical_not(even), row, behind)
            live_ref[i * blocks + e : i * blocks + e + 1, :] = row
    return own


def fill_radial(own, tiles, cols_ref, live_ref, radial_ref):
    xa, ya, za = own
    atoms = xa.shape[1]
    chunk = BLOCK
    for index in range(len(tiles) * atoms // chunk):
        lo = index * chunk
        at = slice(lo, lo + chunk)
        col = cols_ref[at, :]
        dx = col[:, 0:1] - xa
        dy = col[:, 1:2] - ya
        dz = col[:, 2:3] - za
        s = jnp.minimum(dx * dx + dy * dy + dz * dz, 1.0)
        gap = 1.0 - s
        envelope = gap * gap * live_ref[index : index + 1, :]
        if tiles[lo // atoms] == 0:
            other = lax.broadcasted_iota(jnp.int32, (chunk, atoms), 0) + lo
            me = lax.broadcasted_iota(jnp.int32, (chunk, atoms), 1)
            envelope = jnp.where(other == me, 0.0, envelope)
        off = s - MID / (NRAD - 1)
        middle = envelope * jnp.exp(-0.5 * (NRAD - 1) ** 2 * (off * off))
        radial_ref[MID, at, :] = middle.astype(BF)
        grow = jnp.exp((NRAD - 1.0) * s)
        value = middle
        for n in range(MID, NRAD - 1):
            value = value * (grow * math.exp(-(2 * n + 1) / 2))
            radial_ref[n + 1, at, :] = value.astype(BF)
        shrink = jnp.exp((1.0 - NRAD) * s)
        value = middle
        for n in range(MID, 0, -1):
            value = value * (shrink * math.exp((2 * n - 1) / 2))
            radial_ref[n - 1, at, :] = value.astype(BF)


def radial_kernel(
    spaces,
    place_ref,
    own_ref,
    first_ref,
    wave_ref,
    w_rad_ref,
    radial_ref,
    coord_ref,
    filt_ref,
    weight_ref,
    cols_ref,
    live_ref,
):
    atoms = own_ref.shape[1]
    length = SLICE_WIDTH * (atoms // BLOCK) * spaces
    channels = w_rad_ref.shape[1]
    halos = (own_ref, first_ref)
    own = geometry(
        place_ref[0], spaces, halos, (0, 1), channels, cols_ref, live_ref, coord_ref
    )
    w_cols = w_rad_ref[...].T
    for n in range(NRAD):
        filt_ref[n] = jnp.broadcast_to(w_cols[:, n : n + 1], filt_ref.shape[1:])
    fill_radial(own, (0, 1), cols_ref, live_ref, radial_ref)
    weight_ref[...] = mode_weights(wave_ref, length, atoms * spaces)


def radial_other_kernel(
    spaces, place_ref, own_ref, second_ref, filt_ref, radial_ref, coord_ref, cols_ref, live_ref
):
    halos = (own_ref, None, second_ref)
    channels = filt_ref.shape[1]
    own = geometry(place_ref[0], spaces, halos, (2,), channels, cols_ref, live_ref, coord_ref)
    fill_radial(own, (2,), cols_ref, live_ref, radial_ref)


def near_mix(left_ref, radial_ref, radial_other_ref, filt_ref, total_ref):
    cut = radial_ref.shape[1]
    for n in range(NRAD):
        part = dot_nn(left_ref[:, 0:cut], radial_ref[n])
        part = part + dot_nn(left_ref[:, cut:], radial_other_ref[n])
        part = part.reshape(total_ref.shape) * filt_ref[n][None]
        if n == 0:
            total_ref[...] = part
        else:
            total_ref[...] += part


def near_scratch(channels, atoms):
    return [
        pltpu.VMEM((NHARM * channels, 3 * atoms), BF),
        pltpu.VMEM((NHARM, channels, atoms), F32),
    ]


def coord_tile(coord_ref, coord_other_ref, t):
    return coord_ref[t] if t < 2 else coord_other_ref[0]


def coord_rows(coord_ref, coord_other_ref, t):
    tile = coord_tile(coord_ref, coord_other_ref, t)
    return (tile[0:1], tile[1:2], tile[2:3])


def near_grad_kernel(
    own_ref,
    first_ref,
    second_ref,
    radial_ref,
    radial_other_ref,
    coord_ref,
    coord_other_ref,
    filt_ref,
    grad_ref,
    left_ref,
    total_ref,
):
    channels, atoms = grad_ref.shape
    for t, halo in enumerate((own_ref, first_ref, second_ref)):
        at = slice(t * atoms, (t + 1) * atoms)
        valid = coord_tile(coord_ref, coord_other_ref, t)[3:4]
        grads = [
            halo[l * channels : (l + 1) * channels, :].astype(F32) * valid for l in range(NHARM)
        ]
        moved = list(grads)
        for (l, m), term in shift_terms(*coord_rows(coord_ref, coord_other_ref, t)).items():
            moved[m] = moved[m] + grads[l] * term
        for m in range(NHARM):
            left_ref[m * channels : (m + 1) * channels, at] = moved[m].astype(BF)
    near_mix(left_ref, radial_ref, radial_other_ref, filt_ref, total_ref)
    harm = harmonic_rows(*coord_rows(coord_ref, coord_other_ref, 0))
    grad = total_ref[0]
    for m in range(1, NHARM):
        grad = grad + total_ref[m] * harm[m]
    grad_ref[...] = grad


def fill_terms(data, cos, sin, terms_ref, at):
    channels = data.shape[0]
    terms_ref[0:channels, at] = data.astype(BF)
    for k in range(KLONG):
        lo = (1 + 2 * k) * channels
        terms_ref[lo : lo + channels, at] = (data * cos[k : k + 1]).astype(BF)
        terms_ref[lo + channels : lo + 2 * channels, at] = (data * sin[k : k + 1]).astype(BF)


def gathered_sums(fill, pairs, terms_ref, modes_ref):
    span = terms_ref.shape[1]
    group = pairs * span // modes_ref.shape[1]
    sums = None
    for base in range(0, pairs, group):
        lax.fori_loop(0, group, fill, base)
        at = slice(base // group * span, (base // group + 1) * span)
        part = dot_nt(terms_ref[...], modes_ref[:, at])
        sums = part if sums is None else sums + part
    return sums


def far_field(sums, weight_ref, own_ref, own_longs_ref, channels):
    rows_re, rows_im = [], []
    for k in range(KLONG + 1):
        w = weight_ref[k : k + 1, :]
        if k == 0:
            real = sums[0:channels]
            cos, sin = real[:, :KMODE], real[:, KMODE:]
        else:
            lo = (2 * k - 1) * channels
            real, imag = sums[lo : lo + channels], sums[lo + channels : lo + 2 * channels]
            cos = real[:, :KMODE] - imag[:, KMODE:]
            sin = real[:, KMODE:] + imag[:, :KMODE]
        cos, sin = cos * w, sin * w
        rows_re.append(jnp.concatenate([cos, sin], 1))
        if k > 0:
            rows_im.append(jnp.concatenate([sin, -cos], 1))
    waves = jnp.concatenate(rows_re + rows_im, 0).astype(BF)
    back = dot_nn(waves, own_ref[...])
    cos, sin = own_longs_ref[0:8, :], own_longs_ref[8:16, :]
    far = back[0:channels]
    for k in range(KLONG):
        lo = (1 + k) * channels
        far = far + back[lo : lo + channels] * cos[k : k + 1]
        lo = (1 + KLONG + k) * channels
        far = far + back[lo : lo + channels] * sin[k : k + 1]
    return far


def far_scratch(channels, atoms, spaces):
    return [pltpu.VMEM(((2 * KLONG + 1) * channels, min(spaces // 2, 8) * atoms), BF)]


def cot_filler(length, held_ref, channels, modes_ref, longs_ref, terms_ref):
    unit = 2 * channels + 16
    atoms = held_ref.shape[2]

    def fill(p, base):
        for q in range(2):
            lo = q * unit
            tail = held_ref[base + p, lo + channels : lo + channels + 16, :]
            first, second, third = phase_rows(*unpack_pos(tail), length)
            at = pl.ds(pl.multiple_of((2 * (base + p) + q) * atoms, atoms), atoms)
            modes_ref[:, at] = mode_table(second, third)
            longs_ref[0:8, at] = first[0]
            longs_ref[8:16, at] = first[1]
            cot = held_ref[base + p, lo : lo + channels, :].astype(F32)
            at = pl.ds(pl.multiple_of((2 * p + q) * atoms, atoms), atoms)
            fill_terms(cot * tail[10:11].astype(F32), *first, terms_ref, at)
        return base

    return fill


def source_filler(held_ref, channels, longs_ref, terms_ref):
    unit = 2 * channels + 16
    atoms = held_ref.shape[2]

    def fill(p, base):
        for q in range(2):
            lo = q * unit + channels + 16
            data = held_ref[base + p, lo : lo + channels, :].astype(F32)
            at = pl.ds(pl.multiple_of((2 * (base + p) + q) * atoms, atoms), atoms)
            cos, sin = longs_ref[0:8, at], longs_ref[8:16, at]
            at = pl.ds(pl.multiple_of((2 * p + q) * atoms, atoms), atoms)
            fill_terms(data, cos, sin, terms_ref, at)
        return base

    return fill


def half_kernel(
    length,
    held_ref,
    cot_sums_ref,
    source_sums_ref,
    own_ref,
    own_longs_ref,
    terms_ref,
    modes_ref,
    longs_ref,
):
    pairs, rows, atoms = held_ref.shape
    channels = (rows // 2 - 16) // 2
    fill = cot_filler(length, held_ref, channels, modes_ref, longs_ref, terms_ref)
    cot_sums_ref[...] = gathered_sums(fill, pairs, terms_ref, modes_ref)
    fill = source_filler(held_ref, channels, longs_ref, terms_ref)
    source_sums_ref[...] = gathered_sums(fill, pairs, terms_ref, modes_ref)
    own_ref[...] = modes_ref[:, 0:atoms]
    own_longs_ref[...] = longs_ref[:, 0:atoms]


def scaled_kernel(
    length,
    rest_ref,
    near_ref,
    weight_ref,
    gain_ref,
    sums_ref,
    own_ref,
    own_longs_ref,
    order_ref,
    scaled_ref,
    modes_ref,
    longs_ref,
    terms_ref,
):
    channels = near_ref.shape[0]
    fill = cot_filler(length, rest_ref, channels, modes_ref, longs_ref, terms_ref)
    sums = gathered_sums(fill, rest_ref.shape[0], terms_ref, modes_ref) + sums_ref[...]
    far = far_field(sums, weight_ref, own_ref, own_longs_ref, channels)
    scaled_ref[...] = ((near_ref[...] + far) * gain_ref[...]).astype(BF)


def near_messages_kernel(
    own_ref,
    first_ref,
    second_ref,
    radial_ref,
    radial_other_ref,
    coord_ref,
    coord_other_ref,
    filt_ref,
    scalar_ref,
    rest_ref,
    left_ref,
    total_ref,
):
    channels, atoms = scalar_ref.shape
    for t, ref in enumerate((own_ref, first_ref, second_ref)):
        lo = ref.shape[0] - channels
        at = slice(t * atoms, (t + 1) * atoms)
        left_ref[0:channels, at] = ref[lo : lo + channels, :]
        source = ref[lo : lo + channels, :].astype(F32)
        harm = harmonic_rows(*coord_rows(coord_ref, coord_other_ref, t))
        for m in range(1, NHARM):
            left_ref[m * channels : (m + 1) * channels, at] = (source * harm[m]).astype(BF)
    near_mix(left_ref, radial_ref, radial_other_ref, filt_ref, total_ref)
    valid = coord_ref[0][3:4]
    sums = [total_ref[m] for m in range(NHARM)]
    near = list(sums)
    for (l, m), term in shift_terms(*coord_rows(coord_ref, coord_other_ref, 0)).items():
        near[l] = near[l] + sums[m] * term
    scalar_ref[...] = near[0] * valid
    for l in range(1, NHARM):
        rest_ref[l - 1] = (near[l] * valid).astype(BF)


def messages_kernel(
    held_ref,
    scalar_ref,
    rest_ref,
    coord_ref,
    weight_ref,
    sums_ref,
    own_ref,
    own_longs_ref,
    modes_ref,
    longs_ref,
    messages_ref,
    token_ref,
    terms_ref,
):
    channels = scalar_ref.shape[0]
    fill = source_filler(held_ref, channels, longs_ref, terms_ref)
    sums = gathered_sums(fill, held_ref.shape[0], terms_ref, modes_ref) + sums_ref[...]
    far = far_field(sums, weight_ref, own_ref, own_longs_ref, channels)
    valid = coord_ref[0][3:4]
    messages_ref[0] = (scalar_ref[...] + far * valid).astype(BF)
    messages_ref[1:NHARM] = rest_ref[...]
    token_ref[...] = jnp.zeros_like(token_ref)


def final_kernel(chans, lane_ref, w_ref, *refs):
    out_ref, all_ref = refs[-2:]
    channels = out_ref.shape[0]
    lane = lane_ref[0]
    for m, piece in enumerate(refs[:chans]):
        at = pl.multiple_of((lane ^ m) * channels, channels)
        all_ref[pl.ds(at, channels), :] = piece[...]
    first = pl.multiple_of(lane * channels, channels)
    out_ref[...] = dot_nn(w_ref[pl.ds(first, channels), :], all_ref[...])


def cost(micros):
    return pl.CostEstimate(
        flops=int(micros * 1e9), bytes_accessed=int(micros * 3e6), transcendentals=0
    )


def swapped(block, axis, bit):
    return lax.ppermute(block, axis, [(i, i ^ bit) for i in range(lax.axis_size(axis))])


def chan_pieces(raw, kept):
    return [kept] + [swapped(raw, "chan", m) for m in range(1, lax.axis_size("chan"))]


def on_device(
    features,
    positions,
    species,
    block_count,
    pair_home,
    pair_reach,
    pair_count,
    wave_ints,
    species_gain,
    w_in,
    w_rad,
    cotangent,
):
    channels, atoms = features.shape
    spaces = lax.axis_size("space")
    chans = lax.axis_size("chan")
    length = SLICE_WIDTH * (atoms // BLOCK) * spaces
    place = lax.axis_index("space").astype(jnp.int32).reshape(1)
    lane = lax.axis_index("chan").astype(jnp.int32).reshape(1)
    species = species.reshape(1, atoms)
    shape = jax.ShapeDtypeStruct

    def call(kernel, out_shape, smem, vmem, scratch, name, micros):
        return pl.pallas_call(
            kernel,
            out_shape=out_shape,
            in_specs=[SMEM] * len(smem) + [VMEM] * len(vmem),
            out_specs=jax.tree.map(lambda _: VMEM, out_shape),
            scratch_shapes=scratch,
            compiler_params=pltpu.CompilerParams(vmem_limit_bytes=32 * 1024 * 1024),
            cost_estimate=cost(micros),
            name=name,
        )(*smem, *vmem)

    def in_hbm(x):
        return pltpu.with_memory_space_constraint(x, pltpu.HBM)

    cots = cotangent.reshape(NHARM * channels, atoms)
    head, gain, feats_copy, w_copy = pl.pallas_call(
        prep_kernel,
        out_shape=(
            shape((channels + 16, atoms), BF),
            shape((channels, atoms), F32),
            shape(features.shape, BF),
            shape(w_in.shape, BF),
        ),
        in_specs=[SMEM] + [pl.BlockSpec(memory_space=pltpu.HBM)] * 9,
        out_specs=(VMEM,) * 4,
        scratch_shapes=[
            pltpu.SMEM(block_count.shape, jnp.int32),
            pltpu.SMEM(pair_home.shape, jnp.int32),
            pltpu.SMEM(pair_reach.shape, jnp.int32),
            pltpu.VMEM(positions.shape, F32),
            pltpu.VMEM(species.shape, jnp.int32),
            pltpu.VMEM(species_gain.shape, F32),
            pltpu.SemaphoreType.DMA((9,)),
        ],
        compiler_params=pltpu.CompilerParams(vmem_limit_bytes=8 * 1024 * 1024),
        cost_estimate=cost(COST["prep"]),
        name="prep",
    )(
        pair_count,
        *[
            in_hbm(x)
            for x in (
                block_count,
                pair_home,
                pair_reach,
                positions,
                cots,
                species,
                species_gain,
                features,
                w_in,
            )
        ]
    )
    pieces = chan_pieces(features, feats_copy)
    other = [i - 1 if i % 2 == 0 else i + 1 for i in range(spaces)]
    route = [(i, other[i] % spaces) for i in range(spaces)]
    second = lax.ppermute(cots, "space", route)
    first = swapped(cots, "space", 1)
    unit = call(
        functools.partial(source_kernel, chans),
        shape((2 * channels + 16, atoms), BF),
        (lane,),
        (*pieces, w_copy, gain, head, first, second),
        [pltpu.VMEM((w_in.shape[0], atoms), BF), pltpu.VMEM((w_in.shape[1], atoms), F32)],
        "source",
        COST["source"],
    )
    unit_first = swapped(unit, "space", 1)
    unit_second = lax.ppermute(unit[channels:], "space", route)
    block = jnp.concatenate([unit, unit_first], 0)
    held = block[None]
    bit = spaces // 2
    while bit > 2:
        held = jnp.concatenate([held, swapped(held, "space", bit)], 0)
        bit //= 2
    held_rest = swapped(held, "space", 2)
    radial, coord, filt, weight = call(
        functools.partial(radial_kernel, spaces),
        (
            shape((NRAD, 2 * atoms, atoms), BF),
            shape((2, 8, atoms), F32),
            shape((NRAD, channels, atoms), F32),
            shape((16, KMODE), F32),
        ),
        (place,),
        (unit, unit_first, wave_ints, w_rad),
        [pltpu.VMEM((2 * atoms, 8), F32), pltpu.VMEM((16, atoms), F32)],
        "radial",
        COST["radial"],
    )
    radial_other, coord_other = call(
        functools.partial(radial_other_kernel, spaces),
        (shape((NRAD, atoms, atoms), BF), shape((1, 8, atoms), F32)),
        (place,),
        (unit, unit_second, filt),
        [pltpu.VMEM((atoms, 8), F32), pltpu.VMEM((16, atoms), F32)],
        "radial_other",
        1,
    )
    near_grad = call(
        near_grad_kernel,
        shape((channels, atoms), F32),
        (),
        (cots, first, second, radial, radial_other, coord, coord_other, filt),
        near_scratch(channels, atoms),
        "near_grad",
        COST["near_grad"],
    )
    scalar, rest = call(
        near_messages_kernel,
        (shape((channels, atoms), F32), shape((NHARM - 1, channels, atoms), BF)),
        (),
        (unit, unit_first, unit_second, radial, radial_other, coord, coord_other, filt),
        near_scratch(channels, atoms),
        "near_messages",
        COST["near_messages"],
    )
    terms = ((2 * KLONG + 1) * channels, 2 * KMODE)
    table = pltpu.VMEM((2 * KMODE, spaces // 2 * atoms), BF)
    long_rows = pltpu.VMEM((16, spaces // 2 * atoms), F32)
    cot_sums, source_sums, modes_own, longs_own = call(
        functools.partial(half_kernel, length),
        (
            shape(terms, F32),
            shape(terms, F32),
            shape((2 * KMODE, atoms), BF),
            shape((16, atoms), F32),
        ),
        (),
        (held,),
        far_scratch(channels, atoms, spaces) + [table, long_rows],
        "half",
        COST["half"],
    )
    scaled, modes, longs = call(
        functools.partial(scaled_kernel, length),
        (
            shape((channels, atoms), BF),
            shape((2 * KMODE, spaces // 2 * atoms), BF),
            shape((16, spaces // 2 * atoms), F32),
        ),
        (),
        (held_rest, near_grad, weight, gain, cot_sums, modes_own, longs_own, scalar),
        far_scratch(channels, atoms, spaces),
        "scaled",
        COST["scaled"],
    )
    scaled_pieces = chan_pieces(scaled, scaled)
    messages, token = call(
        messages_kernel,
        (shape((NHARM, channels, atoms), BF), shape((8, 128), F32)),
        (),
        (
            held_rest,
            scalar,
            rest,
            coord,
            weight,
            source_sums,
            modes_own,
            longs_own,
            modes,
            longs,
        ),
        far_scratch(channels, atoms, spaces),
        "messages",
        COST["messages"],
    )
    grad_features = call(
        functools.partial(final_kernel, chans),
        shape((channels, atoms), F32),
        (lane,),
        (w_copy, *scaled_pieces, token),
        [pltpu.VMEM((chans * channels, atoms), BF)],
        "final",
        COST["final"],
    )
    return (messages, grad_features)


def mode_weights(wave_ref, length, total):
    k = wave_ref[...]
    count = k.shape[1]
    k = jnp.where(k[0:1] < 0, -k, k)
    k1, k2, k3 = k[0:1], k[1:2], k[2:3]
    code = jnp.where(k3 == 4, 76 + k2, (k2 + 4) * 8 + k3 + 4)
    rows = lax.broadcasted_iota(jnp.int32, (KMODE, count), 0)
    hot = (rows == code).astype(F32).astype(BF)
    longs = lax.broadcasted_iota(jnp.int32, (16, count), 0)
    hot1 = (longs == k1).astype(F32).astype(BF)
    mult = dot_nt(hot1, hot)
    lane = lax.broadcasted_iota(jnp.int32, (16, KMODE), 1)
    row = lax.broadcasted_iota(jnp.int32, (16, KMODE), 0)
    g2 = jnp.where(lane < 72, lane // 8 - 4, lane - 76).astype(F32)
    g3 = jnp.where(lane < 72, lane % 8 - 4, 4).astype(F32)
    f1 = row.astype(F32) * (2.0 * math.pi / length)
    f2 = g2 * (2.0 * math.pi / SIDE_WIDTH)
    f3 = g3 * (2.0 * math.pi / GAP_HEIGHT)
    ksq = f1 * f1 + f2 * f2 + f3 * f3
    value = jnp.exp(-0.5 * ksq) / (ksq + SCREEN * SCREEN) * (1.0 / math.sqrt(count * total))
    return jnp.where(mult > 0.0, mult * value, 0.0)


def phase_rows(x, y, z, length):
    atoms = x.shape[1]
    step = lax.broadcasted_iota(jnp.int32, (8, atoms), 0).astype(F32)
    first = sincos_turns((step + 1.0) * (x * (1.0 / length)))
    second = sincos_turns((step - 4.0) * (y * (1.0 / SIDE_WIDTH)))
    third = sincos_turns((step - 4.0) * (z * (1.0 / GAP_HEIGHT)))
    return first, second, third


def mode_table(second, third):
    c2, s2 = second
    c3, s3 = third
    atoms = c2.shape[1]
    cos, sin = [], []
    for k2 in range(9):
        a = c2[k2 : k2 + 1] if k2 < 8 else c2[0:1]
        b = s2[k2 : k2 + 1] if k2 < 8 else -s2[0:1]
        cos.append(a * c3 - b * s3)
        sin.append(a * s3 + b * c3)
    a, b = c3[0:1], -s3[0:1]
    cos.append(c2 * a - s2 * b)
    sin.append(c2 * b + s2 * a)
    one = lax.broadcasted_iota(jnp.int32, (8, atoms), 0) == 0
    cos.append(jnp.where(one, c2[0:1] * a + s2[0:1] * b, 0.0))
    sin.append(jnp.where(one, c2[0:1] * b - s2[0:1] * a, 0.0))
    pad = jnp.zeros((KMODE - 88, atoms), F32)
    return jnp.concatenate(cos + [pad] + sin + [pad], 0).astype(BF)


def unpack_pos(tail):
    t = tail.astype(F32)
    pos = (t[0:3] + t[3:6]) + t[6:9]
    return pos[0:1], pos[1:2], pos[2:3]


def solution(mesh):
    return jax.shard_map(
        on_device,
        mesh=mesh,
        in_specs=(
            P("chan", "space"),
            P(None, "space"),
            P("space"),
            P("space"),
            P("space"),
            P("space"),
            P("space"),
            P(),
            P(None, "chan"),
            P(),
            P(None, "chan"),
            P(None, "chan", "space"),
        ),
        out_specs=(P(None, "chan", "space"), P("chan", "space")),
        check_vma=False,
    )
```
